32 devices in a mesh: groups: 2 (over x), expert: 16 (over z, y, core).
Axes of the slice: x: 2, y: 2, z: 4, core: 2. Of those that a mesh axis runs over, the one named last changes fastest.
Arguments:
- features: bfloat16 [4096, 256], P(('groups', 'expert')), parts along dimension 0, may hold values from -6 to 6
- scenario_id: int32 [4096], P(('groups', 'expert')), parts along dimension 0, may hold values from 0 to 7, as said below
- scenario_pads: int32 [16], P('groups'), parts along dimension 0, may hold values from 2 to 32, as said below
- device_slot: int32 [16], replicated, may hold values from 0 to 15, as said below
- mentor_raw_predictions: float32 [4096, 128], P(('groups', 'expert')), parts along dimension 0, may hold values from -500 to 500
- gate_weight: bfloat16 [8, 256, 20], replicated, may hold values from -0.375 to 0.375
- common_experts_first_matrix: bfloat16 [16, 256, 1024], P(None, 'expert'), may hold values from -0.375 to 0.375
- shared_reduce: bfloat16 [16, 1024, 256], P(None, 'expert'), may hold values from -0.1875 to 0.1875
- scenario_widen: bfloat16 [16, 256, 2048], P('expert'), may hold values from -0.375 to 0.375
- scenario_narrow: bfloat16 [16, 2048, 256], P('expert'), may hold values from -0.1875 to 0.1875
- head_weight: bfloat16 [256, 128], replicated, may hold values from -0.375 to 0.375
Outputs:
- feature_grad: bfloat16 [4096, 256], P(('groups', 'expert')), parts along dimension 0
- expand_grad: float32 [32, 256, 1024], P('groups', 'expert'), parts along dimension 0
- reduce_grad: float32 [32, 1024, 256], P('groups', 'expert'), parts along dimension 0
- widen_grad: float32 [32, 256, 2048], P(('groups', 'expert')), parts along dimension 0
- narrow_grad: float32 [32, 2048, 256], P(('groups', 'expert')), parts along dimension 0
- gate_grad: float32 [16, 256, 20], P('groups'), parts along dimension 0
- head_grad: float32 [512, 128], P('groups'), parts along dimension 0
The draws below stay inside these ranges and needn't reach their ends.
There are 2 independent parts, one for each index of `groups`. The reference program is written for one: setup_inputs(seed, part) draws one part's arguments, and reference() takes and returns one part's arrays. A program takes and returns all parts, laid end to end along the dimension named above; an argument that names none is the same for every part. Nothing has to cross between parts.
Inputs may be any that keep to these rules, and one draw needn't show every extreme that they name: `scenario_id`: every device holds at least 32 rows of one scenario whose entry of scenario_pads is 32. `scenario_pads`: some entry equals 32. `device_slot`: A permutation; devices 1 i to 1 i + 1 - 1 hold slots 1 m to 1 m + 1 - 1 in this order, for some m.
All inputs are finite; a program needn't handle non-finite values.
Results may differ from the reference program's by a relative error of at most 0.013.
Values may be sent and summed in bfloat16 or wider, within the bound.
No kernel may reach another device: no remote copies, remote signals or barrier semaphores. Data moves between devices by JAX's collectives and lax.ppermute only.
A program may use at most 128 MiB of HBM per device.

```python
import jax
import jax.numpy as jnp
from jax import lax

D = 256
H = 1024
SHARED = 16
SCEN = 8
SE = 4
CLS = 128
ROWS_DEV = 128
TOKENS = 2048
CAP = 32
NG = 20
HC = 2048
SPLIT = 1
N_EXPERT = 16


def permute_rows(piece_key):
    return jax.random.permutation(piece_key, ROWS_DEV)


def scenario_plan(key):
    subkeys = jax.random.split(key, 5)
    weight_table = jax.random.randint(subkeys[0], (SCEN,), 1, 9)
    bounds = jnp.cumsum(weight_table)
    labels = jnp.arange(SCEN)
    pad_values = jax.random.randint(subkeys[1], (SCEN,), 2, CAP + 1)
    busiest = jax.random.randint(subkeys[2], (), 0, SCEN)
    pad_values = jnp.where(labels == busiest, CAP, pad_values)
    raw_values = jax.random.randint(subkeys[3], (N_EXPERT, ROWS_DEV), 0, bounds[-1])
    chosen = jnp.sum(raw_values[:, :, None] >= bounds[None, None, :], axis=2)
    position = jnp.arange(ROWS_DEV)
    chosen = jnp.where(position[None, :] < CAP, busiest, chosen)
    orders = jax.vmap(permute_rows)(jax.random.split(subkeys[4], N_EXPERT))
    chosen = jnp.take_along_axis(chosen, orders, axis=1)
    return (chosen.reshape(N_EXPERT * ROWS_DEV).astype(jnp.int32), pad_values.astype(jnp.int32))


def draw_scenario_id(key, part):
    planned = scenario_plan(key)
    return planned[0]


def draw_scenario_pads(key, part):
    planned = scenario_plan(key)
    return planned[1]


def draw_device_slot(key, part):
    key = jax.random.fold_in(key, 7)
    blocks = jax.random.permutation(key, N_EXPERT // SPLIT)
    position = jnp.arange(N_EXPERT)
    return (blocks[position // SPLIT] * SPLIT + position % SPLIT).astype(jnp.int32)


def draw_mentor_raw_predictions(key, part):
    key = jax.random.fold_in(key, 11)
    subkeys = jax.random.split(key, 1)
    logits = 3.0 * jax.random.normal(subkeys[0], (TOKENS, CLS), jnp.float32)
    logits = jnp.clip(logits, -18.0, 18.0)
    return logits.astype(jnp.float32)


def levels(own_key, dims, cuts, least, high):
    factor_of, own = 1.0, jax.random.fold_in(own_key, 6)
    for dim, shards_of in cuts:
        draws = jnp.exp(jax.random.uniform(jax.random.fold_in(own, dim), (shards_of,), jnp.float32, least / len(cuts), high / len(cuts)))
        factor_of = factor_of * jnp.repeat(draws, dims[dim] // shards_of).reshape([-1 if axis == dim else 1 for axis in range(len(dims))])
    return factor_of


def noise(own_key, dims, deviation, limit, cuts=(), kind=jnp.bfloat16):
    entries = jax.random.normal(own_key, dims, jnp.float32) * deviation
    if len(cuts) > 0:
        entries = levels(own_key, dims, cuts, -0.22, 0.18) * entries
    return jnp.clip(entries, min=-limit, max=limit).astype(kind)


def setup_inputs(seed: int = 0, part: int = 0) -> dict:
    splits = jax.random.split(jax.random.key(seed), 12)
    own_keys = jax.random.split(jax.random.fold_in(splits[11], part), 12)
    return {
        "features": noise(own_keys[0], (TOKENS, D), 1.0, 6.0, ((0, 16),)),
        "scenario_id": draw_scenario_id(jax.random.fold_in(jax.random.fold_in(splits[11], part), 71), part),
        "scenario_pads": draw_scenario_pads(jax.random.fold_in(jax.random.fold_in(splits[11], part), 71), part),
        "device_slot": draw_device_slot(jax.random.fold_in(splits[11], 71), part),
        "mentor_raw_predictions": draw_mentor_raw_predictions(jax.random.fold_in(jax.random.fold_in(splits[11], part), 71), part),
        "gate_weight": noise(splits[5], (SCEN, D, NG), D ** -0.5, 0.375),
        "common_experts_first_matrix": noise(splits[6], (SHARED, D, H), D ** -0.5, 0.375, ((1, 16),)),
        "shared_reduce": noise(splits[7], (SHARED, H, D), H ** -0.5, 0.1875, ((1, 16),)),
        "scenario_widen": noise(splits[8], (N_EXPERT, D, HC), D ** -0.5, 0.375, ((0, 16),)),
        "scenario_narrow": noise(splits[9], (N_EXPERT, HC, D), H ** -0.5, 0.1875, ((0, 16),)),
        "head_weight": noise(splits[10], (D, CLS), D ** -0.5, 0.375),
    }


distillation_warmth = 2.0
highest = lax.Precision.HIGHEST


def silu_slope(affine_response):
    sigmoid = jax.nn.sigmoid(affine_response)
    return sigmoid * (1.0 + affine_response * (1.0 - sigmoid))


def contract(left, right, contraction_axis_index, right_dim):
    return lax.dot_general(left, right, (((contraction_axis_index,), (right_dim,)), ((), ())), preferred_element_type=jnp.float32)


def reference(features, scenario_id, scenario_pads, device_slot, mentor_raw_predictions, gate_weight, common_experts_first_matrix, shared_reduce, scenario_widen, scenario_narrow, head_weight):
    total_per_row = features.shape[0]
    group_size = N_EXPERT // SCEN
    slice_width = scenario_widen.shape[2]
    labels = jnp.arange(SCEN, dtype=jnp.int32)
    onehot = scenario_id[:, None] == labels[None, :]
    flattened_gate = jnp.transpose(gate_weight, (1, 0, 2)).reshape(D, SCEN * NG)
    every_logit = jnp.dot(features, flattened_gate, preferred_element_type=jnp.float32).reshape(total_per_row, SCEN, NG)
    gate_probs = jax.nn.softmax(jnp.sum(jnp.where(onehot[:, :, None], every_logit, 0.0), axis=1), axis=-1)
    gate_round = gate_probs.astype(jnp.bfloat16)

    member = onehot.astype(jnp.int32).reshape(N_EXPERT, ROWS_DEV, SCEN)
    slot_rank = jnp.sum((jnp.cumsum(member, axis=1) - 1) * member, axis=2).reshape(total_per_row).astype(jnp.int32)
    kept_rows = slot_rank < scenario_pads[scenario_id]
    device_of_row = jnp.arange(total_per_row, dtype=jnp.int32) // ROWS_DEV
    slot_total = SCEN * N_EXPERT * CAP
    position = jnp.where(kept_rows, (scenario_id * N_EXPERT + device_of_row) * CAP + slot_rank, slot_total).astype(jnp.int32)
    table = jnp.full((slot_total,), total_per_row, jnp.int32).at[position].set(jnp.arange(total_per_row, dtype=jnp.int32), mode="drop")
    valid = table < total_per_row
    safe_rows = jnp.minimum(table, total_per_row - 1)

    def gather_slots(values):
        picked = jnp.where(valid[:, None], values[safe_rows], jnp.zeros((), values.dtype))
        return picked.reshape(SCEN, N_EXPERT * CAP, values.shape[1])

    def scatter_slots(values):
        width_last = values.shape[-1]
        return jnp.zeros((total_per_row, width_last), jnp.float32).at[table].add(values.reshape(slot_total, width_last), mode="drop")

    owner_of_slot = jnp.argsort(device_slot).astype(jnp.int32)
    widen_all = scenario_widen[owner_of_slot].reshape(SCEN, group_size, D, slice_width).transpose(0, 2, 1, 3).reshape(SCEN, D, SE * H)
    narrow_all = scenario_narrow[owner_of_slot].reshape(SCEN, SE, H, D)
    slot_rows = gather_slots(features)
    slot_gates = gather_slots(gate_round[:, SHARED:])

    def scenario_forward(rows_in, widen, narrow):
        affine_response = jnp.dot(rows_in, widen, preferred_element_type=jnp.float32)
        active = jax.nn.silu(affine_response).astype(jnp.bfloat16)
        outputs = jnp.einsum("mjh,jhd->mjd", active.reshape(-1, SE, H).astype(jnp.float32), narrow.astype(jnp.float32), precision=highest)
        return affine_response, active, outputs

    def scenario_mix(operands):
        rows_in, gates_in, widen, narrow = operands
        affine_response, active, outputs = scenario_forward(rows_in, widen, narrow)
        return jnp.sum(gates_in.astype(jnp.float32)[:, :, None] * outputs, axis=1)

    routed = scatter_slots(lax.map(scenario_mix, (slot_rows, slot_gates, widen_all, narrow_all)))

    def shared_step(total, operands):
        expand, shrink, column = operands
        active = jax.nn.silu(jnp.dot(features, expand, preferred_element_type=jnp.float32)).astype(jnp.bfloat16)
        output = jnp.dot(active, shrink, preferred_element_type=jnp.float32)
        return total + column.astype(jnp.float32)[:, None] * output, output

    shared_mix, expert_outputs = lax.scan(shared_step, jnp.zeros((total_per_row, D), jnp.float32), (common_experts_first_matrix, shared_reduce, gate_round[:, :SHARED].T))
    layer_output = shared_mix + routed
    layer_round = layer_output.astype(jnp.bfloat16)
    learner_raw_predictions = jnp.dot(layer_round, head_weight, preferred_element_type=jnp.float32)
    prediction_derivative = (distillation_warmth * (jax.nn.softmax(learner_raw_predictions / distillation_warmth, axis=-1) - jax.nn.softmax(mentor_raw_predictions / distillation_warmth, axis=-1))).astype(jnp.bfloat16)
    head_grad = contract(layer_round, prediction_derivative, 0, 0)
    output_grad = contract(prediction_derivative, head_weight, 1, 1)
    output_round = output_grad.astype(jnp.bfloat16)
    output_wide = output_round.astype(jnp.float32)
    shared_dots = jnp.einsum("td,ktd->tk", output_wide, expert_outputs, precision=highest)

    def shared_back(total, operands):
        expand, shrink, column = operands
        affine_response = jnp.dot(features, expand, preferred_element_type=jnp.float32)
        active = jax.nn.silu(affine_response).astype(jnp.bfloat16)
        cotangent = (column.astype(jnp.float32)[:, None] * output_wide).astype(jnp.bfloat16)
        hidden_grad = contract(cotangent, shrink, 1, 1)
        linear_grad = (hidden_grad * silu_slope(affine_response)).astype(jnp.bfloat16)
        return total + contract(linear_grad, expand, 1, 1), (contract(features, linear_grad, 0, 0), contract(active, cotangent, 0, 0))

    common_grad, (expand_grad, reduce_grad) = lax.scan(shared_back, jnp.zeros((total_per_row, D), jnp.float32), (common_experts_first_matrix, shared_reduce, gate_round[:, :SHARED].T))

    slot_cotangents = gather_slots(output_round)

    def scenario_back(operands):
        rows_in, gates_in, widen, narrow, slot_cotangent = operands
        affine_response, active, outputs = scenario_forward(rows_in, widen, narrow)
        cotangent_wide = slot_cotangent.astype(jnp.float32)
        gates_wide = gates_in.astype(jnp.float32)
        dots = jnp.einsum("md,mjd->mj", cotangent_wide, outputs, precision=highest)
        hidden_grad = jnp.einsum("md,jhd->mjh", cotangent_wide, narrow.astype(jnp.float32), precision=highest)
        linear_grad = ((gates_wide[:, :, None] * hidden_grad).reshape(-1, SE * H) * silu_slope(affine_response)).astype(jnp.bfloat16)
        gated_active = (gates_wide[:, :, None] * active.reshape(-1, SE, H).astype(jnp.float32)).astype(jnp.bfloat16)
        narrow_part = jnp.einsum("mjh,md->jhd", gated_active.astype(jnp.float32), cotangent_wide, precision=highest)
        widen_part = contract(rows_in, linear_grad, 0, 0)
        return contract(linear_grad, widen, 1, 1), dots, widen_part, narrow_part

    slot_input, slot_dots, widen_slots, narrow_slots = lax.map(scenario_back, (slot_rows, slot_gates, widen_all, narrow_all, slot_cotangents))
    routed_grad = scatter_slots(slot_input)
    routed_dots = scatter_slots(slot_dots)
    widen_grad = widen_slots.reshape(SCEN, D, group_size, slice_width).transpose(0, 2, 1, 3).reshape(N_EXPERT, D, slice_width)[device_slot]
    narrow_grad = narrow_slots.reshape(N_EXPERT, slice_width, D)[device_slot]

    mix_grad = jnp.concatenate([shared_dots, routed_dots], axis=1)
    score_gradient = gate_probs * (mix_grad - jnp.sum(gate_probs * mix_grad, axis=1, keepdims=True))
    score_round = score_gradient.astype(jnp.bfloat16)
    score_wide = jnp.where(onehot[:, :, None], score_round[:, None, :], jnp.zeros((), jnp.bfloat16)).reshape(total_per_row, SCEN * NG)
    gate_grad = jnp.transpose(contract(features, score_wide, 0, 0).reshape(D, SCEN, NG), (1, 0, 2))
    gate_input = contract(score_wide, flattened_gate, 1, 1)
    feature_grad = (common_grad + routed_grad + gate_input).astype(jnp.bfloat16)
    return (feature_grad, expand_grad, reduce_grad, widen_grad, narrow_grad, gate_grad, head_grad)
```

```python
import functools

import jax
import jax.numpy as jnp
from jax import lax
from jax.experimental import pallas as pl
from jax.experimental.pallas import tpu as pltpu
from jax.sharding import PartitionSpec as P

AXIS = "expert"
TILE = 256
AUX = 32
bf16 = jnp.bfloat16
f32 = jnp.float32


def mm(left, right, left_dim=1, right_dim=0):
    return lax.dot_general(
        left, right, (((left_dim,), (right_dim,)), ((), ())), preferred_element_type=f32
    )


def call(kernel, out_shapes, operands, in_specs=None, scratch=(), flops=0, nbytes=0, limit=48):
    specs = in_specs or [None] * len(operands)
    specs = [pl.BlockSpec(memory_space=pltpu.VMEM) if s is None else s for s in specs]
    return pl.pallas_call(
        kernel,
        out_shape=out_shapes,
        in_specs=specs,
        out_specs=[pl.BlockSpec(memory_space=pltpu.VMEM) for _ in out_shapes],
        scratch_shapes=list(scratch),
        compiler_params=pltpu.CompilerParams(vmem_limit_bytes=limit * 1024 * 1024),
        cost_estimate=pl.CostEstimate(flops=flops, bytes_accessed=nbytes, transcendentals=0),
    )(*operands)


SCALARS = pl.BlockSpec(memory_space=pltpu.SMEM)


def struct(shape, kind):
    return jax.ShapeDtypeStruct(shape, kind)


def sigmoid(v):
    return 0.5 * (1.0 + jnp.tanh(0.5 * v))


def eye(size):
    rows = lax.broadcasted_iota(jnp.int32, (size, size), 0)
    cols = lax.broadcasted_iota(jnp.int32, (size, size), 1)
    return (rows == cols).astype(f32).astype(bf16)


def spread(tile, expert_lanes):
    rows = lax.broadcasted_iota(jnp.int32, (AUX, TILE), 0)
    lanes = lax.broadcasted_iota(jnp.int32, (AUX, TILE), 1) + tile * TILE
    first = rows * expert_lanes
    return ((lanes >= first) & (lanes < first + expert_lanes)).astype(f32).astype(bf16)


def side_of(piece):
    half = piece.shape[1] // 2
    return jnp.concatenate([piece[:, :half], piece[:, half:]], axis=0)


def selector(side, gate_count, scenario, capacity):
    wide = side.astype(f32)
    which = wide[gate_count : gate_count + 1, :]
    slot = wide[gate_count + 1 : gate_count + 2, :]
    ranks = lax.broadcasted_iota(jnp.int32, (capacity, side.shape[1]), 0).astype(f32)
    hit = (ranks == slot) & (which == scenario.astype(f32))
    return hit.astype(f32).astype(bf16)


def prep_kernel(gate_count, capacity, pads, feats, sid, gate_rows, pack, probs, scr):
    rows = feats.shape[0]
    scenarios = gate_rows.shape[0] // AUX
    x = feats[...]
    logits = mm(gate_rows[...], x, 1, 1)
    own = jnp.zeros((AUX, rows), f32)
    ids = sid[...]
    pad = jnp.zeros((1, rows), f32)
    for s in range(scenarios):
        hit = ids == s
        own = own + jnp.where(hit, logits[s * AUX : (s + 1) * AUX], 0.0)
        pad = pad + jnp.where(hit, pads[s].astype(f32), 0.0)
    live = lax.broadcasted_iota(jnp.int32, (AUX, rows), 0) < gate_count
    own = jnp.where(live, own, -jnp.inf)
    top = jnp.max(own, axis=0, keepdims=True)
    raised = jnp.exp(own - top)
    share = raised / jnp.sum(raised, axis=0, keepdims=True)
    probs[...] = share
    labels = lax.broadcasted_iota(jnp.int32, (AUX, rows), 0)
    member = (ids == labels).astype(f32)
    earlier = (
        lax.broadcasted_iota(jnp.int32, (rows, rows), 0)
        < lax.broadcasted_iota(jnp.int32, (rows, rows), 1)
    ).astype(f32).astype(bf16)
    rank = jnp.sum(mm(member.astype(bf16), earlier) * member, axis=0, keepdims=True)
    slot = jnp.where(rank < pad, rank, -1.0)
    scr[...] = share
    scr[gate_count : gate_count + 1, :] = ids.astype(f32)
    scr[gate_count + 1 : gate_count + 2, :] = slot
    side = scr[...].astype(bf16)
    pack[:rows, :] = x
    pack[rows:, :rows] = side[: AUX // 2]
    pack[rows:, rows:] = side[AUX // 2 :]


def compact_kernel(n, gate_count, capacity, with_gates, scal, *refs):
    sides, values, outs = refs[:n], refs[n : 2 * n], refs[2 * n :]
    m = values[0].shape[0]
    rows = sides[0].shape[1] - AUX // 2
    for k in range(n):
        for b in range(m):
            side = side_of(sides[k][b, sides[k].shape[1] - AUX // 2 :, :])
            at = (k * m + b) * capacity
            value = values[k][b, :rows, :]
            for which, out in enumerate(outs):
                sel = selector(side, gate_count, scal[which], capacity)
                width = value.shape[1]
                out[at : at + capacity, :width] = mm(sel, value).astype(bf16)
                if with_gates:
                    out[at : at + capacity, width : width + AUX] = mm(sel, side, 1, 1).astype(bf16)
                    out[at : at + capacity, width + AUX :] = jnp.zeros(
                        (capacity, out.shape[1] - width - AUX), bf16
                    )


def chosen_gate(x, width, column):
    gates = x[:, width:].astype(f32)
    lanes = lax.broadcasted_iota(jnp.int32, gates.shape, 1)
    return jnp.sum(jnp.where(lanes == column, gates, 0.0), axis=1, keepdims=True)


def scenario_forward_kernel(shared, span, scal, own, other, widen, narrow, out_own, out_other, xs, gated):
    half, width = out_own.shape
    total = widen.shape[1]
    xs[:half, :] = own[...]
    xs[half:, :] = other[...]
    chunk = min(2 * half, 512)

    def tile(j, _):
        lanes = pl.ds(pl.multiple_of(j * TILE, TILE), TILE)
        column = shared + scal[2] + (j * TILE) // span
        for at in range(0, 2 * half, chunk):
            x = xs[at : at + chunk, :]
            linear = mm(x[:, :width], widen[:, lanes])
            active = (linear * sigmoid(linear)).astype(bf16).astype(f32)
            gated[at : at + chunk, lanes] = (chosen_gate(x, width, column) * active).astype(bf16)
        return 0

    lax.fori_loop(0, total // TILE, tile, 0)
    out_own[...] = mm(gated[:half, :], narrow[...]).astype(bf16)
    out_other[...] = mm(gated[half:, :], narrow[...]).astype(bf16)


def unpack(pieces, rows, fs, gs):
    n, m = len(pieces), pieces[0].shape[0]
    for k in range(n):
        for b in range(m):
            at = (k * m + b) * rows
            fs[at : at + rows, :] = pieces[k][b, :rows, :]
            gs[at : at + rows, :] = mm(side_of(pieces[k][b, rows:, :]), eye(AUX), 0, 0).astype(bf16)


def shared_forward_kernel(n, gate_count, capacity, expert_lanes, scal, *refs):
    pieces = refs[:n]
    w1, w2, from_own, from_other = refs[n : n + 4]
    outs = refs[n + 4 : 2 * n + 4]
    fs, gs, gated = refs[2 * n + 4 :]
    m, rows, _ = outs[0].shape
    unpack(pieces, rows, fs, gs)
    total = n * m * rows
    chunk = min(total, 1024)

    def tile(j, _):
        lanes = pl.ds(pl.multiple_of(j * TILE, TILE), TILE)
        for at in range(0, total, chunk):
            linear = mm(fs[at : at + chunk, :], w1[:, lanes])
            active = linear * sigmoid(linear)
            gate = mm(gs[at : at + chunk, :], spread(j, expert_lanes))
            gated[at : at + chunk, lanes] = (gate * active).astype(bf16)
        return 0

    lax.fori_loop(0, w1.shape[1] // TILE, tile, 0)
    for at in range(0, total, chunk):
        mixed = mm(gated[at : at + chunk, :], w2[...])
        for piece in range(at // rows, (at + chunk) // rows):
            k, b = piece // m, piece % m
            side = side_of(pieces[k][b, rows:, :])
            slots = slice(piece * capacity, (piece + 1) * capacity)
            extra = mm(selector(side, gate_count, scal[0], capacity), from_own[slots, :], 0, 0)
            extra += mm(selector(side, gate_count, scal[1], capacity), from_other[slots, :], 0, 0)
            outs[k][b] = (mixed[piece * rows - at : (piece + 1) * rows - at] + extra).astype(bf16)


def softmax(v):
    raised = jnp.exp(v - jnp.max(v, axis=1, keepdims=True))
    return raised / jnp.sum(raised, axis=1, keepdims=True)


def head_kernel(count, *refs):
    parts = refs[:count]
    head, mentor, grad, head_part = refs[count:]
    layer = parts[0][...].astype(f32)
    for part in parts[1:]:
        layer = layer + part[...].astype(f32)
    rounded = layer.astype(bf16)
    student = mm(rounded, head[...])
    value = (2.0 * (softmax(student * 0.5) - softmax(mentor[...] * 0.5))).astype(bf16)
    grad[...] = value
    head_part[...] = mm(rounded, value, 0, 0)


def shared_backward_kernel(n, expert_lanes, *refs):
    pieces, logits = refs[:n], refs[n : 2 * n]
    head, w1, w2, dx, mix, dw1, dw2, fs, gs, os, linear_grad = refs[2 * n :]
    m, rows, _ = logits[0].shape
    unpack(pieces, rows, fs, gs)
    for k in range(n):
        for b in range(m):
            at = (k * m + b) * rows
            os[at : at + rows, :] = mm(logits[k][b], head[...], 1, 1).astype(bf16)
    total = n * m * rows
    chunk = min(total, 1024)
    mix[...] = jnp.zeros_like(mix)

    def tile(j, _):
        lanes = pl.ds(pl.multiple_of(j * TILE, TILE), TILE)
        picks = spread(j, expert_lanes)
        for at in range(0, total, chunk):
            x = fs[at : at + chunk, :]
            cotangent = os[at : at + chunk, :]
            linear = mm(x, w1[:, lanes])
            sig = sigmoid(linear)
            active = linear * sig
            gate = mm(gs[at : at + chunk, :], picks)
            hidden = mm(cotangent, w2[lanes, :], 1, 1)
            mix[at : at + chunk, :] += mm((active * hidden).astype(bf16), picks, 1, 1)
            slope = sig + active * (1.0 - sig)
            grad = (gate * hidden * slope).astype(bf16)
            linear_grad[at : at + chunk, lanes] = grad
            first = mm(x, grad, 0, 0)
            second = mm((gate * active).astype(bf16), cotangent, 0, 0)
            if at == 0:
                dw1[:, lanes] = first
                dw2[lanes, :] = second
            else:
                dw1[:, lanes] += first
                dw2[lanes, :] += second
        return 0

    lax.fori_loop(0, w1.shape[1] // TILE, tile, 0)
    for at in range(0, total, chunk):
        dx[at : at + chunk, :] = mm(linear_grad[at : at + chunk, :], w1[...], 1, 1)


def scenario_backward_kernel(
    shared, span, scal, own, other, logit_own, logit_other, head, widen, narrow,
    out_own, out_other, dwiden, dnarrow, xs, os, linear_grad, mix,
):
    half = out_own.shape[0]
    width = narrow.shape[1]
    total = widen.shape[1]
    xs[:half, :] = own[...]
    xs[half:, :] = other[...]
    os[:half, :] = mm(logit_own[...], head[...], 1, 1).astype(bf16)
    os[half:, :] = mm(logit_other[...], head[...], 1, 1).astype(bf16)
    mix[...] = jnp.zeros_like(mix)
    chunk = min(2 * half, 512)

    def tile(j, _):
        lanes = pl.ds(pl.multiple_of(j * TILE, TILE), TILE)
        column = shared + scal[2] + (j * TILE) // span
        picks = (
            lax.broadcasted_iota(jnp.int32, (TILE, mix.shape[1]), 1) == column
        ).astype(f32).astype(bf16)
        for at in range(0, 2 * half, chunk):
            x = xs[at : at + chunk, :]
            gate = chosen_gate(x, width, column)
            x = x[:, :width]
            cotangent = os[at : at + chunk, :]
            linear = mm(x, widen[:, lanes])
            sig = sigmoid(linear)
            active = (linear * sig)
            hidden = mm(cotangent, narrow[lanes, :], 1, 1)
            mix[at : at + chunk, :] += mm((active * hidden).astype(bf16), picks)
            slope = sig + active * (1.0 - sig)
            grad = (gate * hidden * slope).astype(bf16)
            linear_grad[at : at + chunk, lanes] = grad
            first = mm(x, grad, 0, 0)
            second = mm((gate * active).astype(bf16), cotangent, 0, 0)
            if at == 0:
                dwiden[:, lanes] = first
                dnarrow[lanes, :] = second
            else:
                dwiden[:, lanes] += first
                dnarrow[lanes, :] += second
        return 0

    lax.fori_loop(0, total // TILE, tile, 0)
    for at, out in ((0, out_own), (half, out_other)):
        out[:, :width] = mm(linear_grad[at : at + half, :], widen[...], 1, 1).astype(bf16)
        out[:, width:] = mix[at : at + half, :].astype(bf16)


def scatter_kernel(n, gate_count, capacity, scal, *refs):
    sides = refs[:n]
    dx, mix, from_own, from_other = refs[n : n + 4]
    outs = refs[n + 4 :]
    m, width = outs[0].shape[0], outs[0].shape[2]
    rows = dx.shape[0] // (n * m)
    for k in range(n):
        for b in range(m):
            piece = k * m + b
            side = side_of(sides[k][b, sides[k].shape[1] - AUX // 2 :, :])
            slots = slice(piece * capacity, (piece + 1) * capacity)
            extra = mm(selector(side, gate_count, scal[0], capacity), from_own[slots, :], 0, 0)
            extra += mm(selector(side, gate_count, scal[1], capacity), from_other[slots, :], 0, 0)
            span = slice(piece * rows, (piece + 1) * rows)
            outs[k][b, :rows, :] = (dx[span, :] + extra[:, :width]).astype(bf16)
            dots = (mix[span, :] + extra[:, width : width + AUX]).astype(bf16)
            turned = mm(eye(AUX), dots, 1, 1).astype(bf16)
            outs[k][b, rows:, :rows] = turned[: AUX // 2]
            outs[k][b, rows:, rows:] = turned[AUX // 2 :]


def final_kernel(count, gate_count, *refs):
    parts = refs[:count]
    feats, sid, probs, gate_rows, out, gate_part, wide = refs[count:]
    rows = feats.shape[0]
    total = parts[0][...].astype(f32)
    for part in parts[1:]:
        total = total + part[...].astype(f32)
    tail = total[rows:]
    half = tail.shape[1] // 2
    dots = jnp.concatenate([tail[:, :half], tail[:, half:]], axis=0)
    share = probs[...]
    live = lax.broadcasted_iota(jnp.int32, (AUX, rows), 0) < gate_count
    dots = jnp.where(live, dots, 0.0)
    score = share * (dots - jnp.sum(share * dots, axis=0, keepdims=True))
    score = score.astype(bf16).astype(f32)
    ids = sid[...]
    for s in range(gate_rows.shape[0] // AUX):
        wide[s * AUX : (s + 1) * AUX, :] = jnp.where(ids == s, score, 0.0).astype(bf16)
    gate_part[...] = mm(wide[...], feats[...])
    out[...] = (total[:rows] + mm(wide[...], gate_rows[...], 0, 0)).astype(bf16)


def body(
    features,
    scenario_id,
    scenario_pads,
    device_slot,
    mentor,
    gate_weight,
    expand,
    reduce,
    scenario_widen,
    scenario_narrow,
    head,
):
    rows, width = features.shape
    devices = lax.axis_size(AXIS)
    index = lax.axis_index(AXIS)
    core = index % 2
    chips = devices // 2
    near = 2 ** ((chips.bit_length() - 1) // 2)
    far = chips // near
    flat = chips <= 8
    n, m = (chips, 1) if flat else (near, far)
    shared, depth, hidden = expand.shape
    lanes = hidden // chips
    scenarios, _, gates = gate_weight.shape
    capacity = rows // 4
    group = devices // scenarios
    slot_width = scenario_widen.shape[2]
    span = min(hidden, slot_width)
    classes = head.shape[1]
    all_rows = chips * rows
    slots = chips * capacity
    hidden_chip = shared * lanes
    groups = [[2 * r + c for r in range(chips)] for c in range(2)]

    def send(value, mask):
        return lax.ppermute(value, AXIS, [(i, i ^ mask) for i in range(devices)])

    def gather(value):
        column = [value] + [send(value, 2 * near * b) for b in range(1, far)]
        if flat:
            out = []
            for b in range(far):
                out += [column[b][None]] + [send(column[b], 2 * a)[None] for a in range(1, near)]
            return out
        stacked = jnp.stack(column)
        return [stacked] + [send(stacked, 2 * a) for a in range(1, near)]

    def scatter(parts):
        if flat:
            column = []
            for b in range(far):
                total = parts[b * near][0].astype(f32)
                for a in range(1, near):
                    total = total + send(parts[b * near + a][0], 2 * a).astype(f32)
                column.append(total if b == 0 else total.astype(bf16))
        else:
            total = parts[0].astype(f32)
            for a in range(1, near):
                total = total + send(parts[a], 2 * a).astype(f32)
            column = [total[0]] + [total[b].astype(bf16) for b in range(1, far)]
        return [column[0]] + [send(column[b], 2 * near * b) for b in range(1, far)]

    def total_of(value):
        mask = 1
        while mask < devices:
            value = value + send(value, mask)
            mask *= 2
        return value

    def ordered(mine, theirs):
        return jnp.where(core == 0, mine, theirs), jnp.where(core == 0, theirs, mine)

    own_slot = lax.dynamic_index_in_dim(device_slot, index, keepdims=False)
    other_slot = lax.dynamic_index_in_dim(device_slot, index ^ 1, keepdims=False)
    first_expert = own_slot % group * slot_width // hidden
    scal = jnp.stack([own_slot // group, other_slot // group, first_expert]).astype(jnp.int32)
    sid = scenario_id.reshape(1, rows)
    gate_rows = jnp.pad(
        jnp.transpose(gate_weight, (0, 2, 1)), ((0, 0), (0, AUX - gates), (0, 0))
    ).reshape(scenarios * AUX, width)
    widen, narrow = scenario_widen[0], scenario_narrow[0]

    pieces = expand.reshape(shared, depth, chips, lanes).transpose(2, 0, 1, 3)
    pieces = lax.all_to_all(
        pieces, AXIS, split_axis=0, concat_axis=0, tiled=True, axis_index_groups=groups
    )
    low, high = ordered(pieces, send(pieces, 1))
    w1 = jnp.stack([low, high]).transpose(1, 0, 3, 2, 4).reshape(width, hidden_chip)
    low, high = ordered(reduce, send(reduce, 1))
    w2 = jnp.stack([low, high], axis=1).reshape(hidden_chip, width)

    pack_rows = rows + AUX // 2
    pack, probs = call(
        functools.partial(prep_kernel, gates, capacity),
        [struct((pack_rows, width), bf16), struct((AUX, rows), f32)],
        [scenario_pads, features, sid, gate_rows],
        [SCALARS, None, None, None],
        [pltpu.VMEM((AUX, rows), f32)],
    )
    got = gather(pack)

    def compact(values, value_width, with_gates):
        out_width = value_width + 128 * with_gates
        return call(
            functools.partial(compact_kernel, n, gates, capacity, with_gates),
            [struct((slots, out_width), bf16)] * 2,
            [scal, *got, *values],
            [SCALARS] + [None] * (2 * n),
        )

    x_own, x_send = compact(got, width, True)
    x_other = send(x_send, 1)
    scen_flops = 4 * slots * width * slot_width
    out_own, out_send = call(
        functools.partial(scenario_forward_kernel, shared, span),
        [struct((slots, width), bf16)] * 2,
        [scal, x_own, x_other, widen, narrow],
        [SCALARS] + [None] * 4,
        [pltpu.VMEM((2 * slots, width + 128), bf16), pltpu.VMEM((2 * slots, slot_width), bf16)],
        flops=2 * scen_flops,
    )
    out_other = send(out_send, 1)
    shared_flops = 2 * all_rows * width * hidden_chip
    row_scratch = [pltpu.VMEM((all_rows, width), bf16), pltpu.VMEM((all_rows, AUX), bf16)]
    parts = call(
        functools.partial(shared_forward_kernel, n, gates, capacity, lanes),
        [struct((m, rows, width), bf16)] * n,
        [scal, *got, w1, w2, out_own, out_other],
        [SCALARS] + [None] * (n + 4),
        row_scratch + [pltpu.VMEM((all_rows, hidden_chip), bf16)],
        flops=2 * shared_flops,
    )
    layer_parts = scatter(parts)
    logit_grad, head_part = call(
        functools.partial(head_kernel, len(layer_parts)),
        [struct((rows, classes), bf16), struct((width, classes), f32)],
        [*layer_parts, head, mentor],
    )
    logits = gather(logit_grad)
    head_total = total_of(head_part)

    l_own, l_send = compact(logits, classes, False)
    l_other = send(l_send, 1)
    dx, mix, dw1, dw2 = call(
        functools.partial(shared_backward_kernel, n, lanes),
        [
            struct((all_rows, width), f32),
            struct((all_rows, AUX), f32),
            struct((width, hidden_chip), f32),
            struct((hidden_chip, width), f32),
        ],
        [*got, *logits, head, w1, w2],
        None,
        row_scratch
        + [pltpu.VMEM((all_rows, width), bf16), pltpu.VMEM((all_rows, hidden_chip), bf16)],
        flops=5 * shared_flops,
    )
    dw1 = dw1.reshape(chips, 2, depth, shared, lanes)
    kept = lax.dynamic_index_in_dim(dw1, core, 1, False)
    sent = lax.dynamic_index_in_dim(dw1, 1 - core, 1, False).astype(bf16)
    dw1 = (kept + send(sent, 1).astype(f32)).astype(bf16)
    dw1 = lax.all_to_all(
        dw1, AXIS, split_axis=0, concat_axis=0, tiled=True, axis_index_groups=groups
    )
    expand_grad = dw1.transpose(2, 1, 0, 3).reshape(shared, depth, hidden).astype(f32)
    dw2 = dw2.reshape(shared, 2, lanes // 2, width)
    kept = lax.dynamic_index_in_dim(dw2, core, 1, False)
    sent = lax.dynamic_index_in_dim(dw2, 1 - core, 1, False).astype(bf16)
    reduce_grad = kept + send(sent, 1).astype(f32)

    dx_own, dx_send, widen_grad, narrow_grad = call(
        functools.partial(scenario_backward_kernel, shared, span),
        [struct((slots, width + 128), bf16)] * 2
        + [struct((width, slot_width), f32), struct((slot_width, width), f32)],
        [scal, x_own, x_other, l_own, l_other, head, widen, narrow],
        [SCALARS] + [None] * 7,
        [
            pltpu.VMEM((2 * slots, width + 128), bf16),
            pltpu.VMEM((2 * slots, width), bf16),
            pltpu.VMEM((2 * slots, slot_width), bf16),
            pltpu.VMEM((2 * slots, 128), f32),
        ],
        flops=5 * scen_flops,
    )
    dx_other = send(dx_send, 1)
    grad_parts = call(
        functools.partial(scatter_kernel, n, gates, capacity),
        [struct((m, pack_rows, width), bf16)] * n,
        [scal, *got, dx, mix, dx_own, dx_other],
        [SCALARS] + [None] * (n + 4),
    )
    grad_parts = scatter(grad_parts)
    feature_grad, gate_part = call(
        functools.partial(final_kernel, len(grad_parts), gates),
        [struct((rows, width), bf16), struct((scenarios * AUX, width), f32)],
        [*grad_parts, features, sid, probs, gate_rows],
        None,
        [pltpu.VMEM((scenarios * AUX, rows), bf16)],
    )
    gate_part = gate_part.reshape(scenarios, AUX, width)[:, :gates]
    gate_total = jnp.transpose(total_of(gate_part), (0, 2, 1))
    return (
        feature_grad,
        expand_grad,
        reduce_grad,
        widen_grad[None],
        narrow_grad[None],
        gate_total,
        head_total,
    )


def solution(mesh):
    placed = (
        P(("groups", "expert"), None),
        P(("groups", "expert")),
        P("groups"),
        P(),
        P(("groups", "expert"), None),
        P(),
        P(None, "expert", None),
        P(None, "expert", None),
        P("expert", None, None),
        P("expert", None, None),
        P(),
    )
    return jax.shard_map(
        body,
        mesh=mesh,
        in_specs=placed,
        out_specs=(
            P(("groups", "expert"), None),
            P("groups", "expert", None),
            P("groups", "expert", None),
            P(("groups", "expert"), None, None),
            P(("groups", "expert"), None, None),
            P("groups", None, None),
            P("groups", None),
        ),
        check_vma=False,
    )
```

```python
import functools

import jax
import jax.numpy as jnp
from jax import lax
from jax.experimental import pallas as pl
from jax.experimental.pallas import tpu as pltpu
from jax.sharding import PartitionSpec as P

AXIS = "expert"
TILE = 256
AUX = 32
bf16 = jnp.bfloat16
f32 = jnp.float32
CHUNK = 256
SMALL, BIG = 24, 32


def mm(left, right, left_dim=1, right_dim=0):
    return lax.dot_general(
        left, right, (((left_dim,), (right_dim,)), ((), ())), preferred_element_type=f32
    )


def call(kernel, out_shapes, operands, in_specs=None, scratch=(), flops=0, nbytes=0, limit=48):
    specs = in_specs or [None] * len(operands)
    specs = [pl.BlockSpec(memory_space=pltpu.VMEM) if s is None else s for s in specs]
    return pl.pallas_call(
        kernel,
        out_shape=out_shapes,
        in_specs=specs,
        out_specs=[pl.BlockSpec(memory_space=pltpu.VMEM) for _ in out_shapes],
        scratch_shapes=list(scratch),
        compiler_params=pltpu.CompilerParams(vmem_limit_bytes=limit * 1024 * 1024),
        cost_estimate=pl.CostEstimate(flops=flops, bytes_accessed=nbytes, transcendentals=0),
    )(*operands)


SCALARS = pl.BlockSpec(memory_space=pltpu.SMEM)


def struct(shape, kind):
    return jax.ShapeDtypeStruct(shape, kind)


def sigmoid(v):
    return 0.5 * (1.0 + jnp.tanh(0.5 * v))


def eye(size):
    rows = lax.broadcasted_iota(jnp.int32, (size, size), 0)
    cols = lax.broadcasted_iota(jnp.int32, (size, size), 1)
    return (rows == cols).astype(f32).astype(bf16)


def spread(tile, expert_lanes):
    rows = lax.broadcasted_iota(jnp.int32, (AUX, TILE), 0)
    lanes = lax.broadcasted_iota(jnp.int32, (AUX, TILE), 1) + tile * TILE
    first = rows * expert_lanes
    return ((lanes >= first) & (lanes < first + expert_lanes)).astype(f32).astype(bf16)


def turn_matrix(size, depth, core):
    place = lax.broadcasted_iota(jnp.int32, (size, size), 0)
    column = lax.broadcasted_iota(jnp.int32, (size, size), 1)
    half = size // 2
    other = place // half
    place = place - other * half
    chip = place // depth
    which = jnp.where(core == 0, other, 1 - other)
    return (column == (chip * 2 + which) * depth + (place - chip * depth)).astype(f32).astype(bf16)


def side_of(piece):
    half = piece.shape[1] // 2
    return jnp.concatenate([piece[:, :half], piece[:, half:]], axis=0)


def selector(side, gate_count, scenario, capacity):
    wide = side.astype(f32)
    which = wide[gate_count : gate_count + 1, :]
    slot = wide[gate_count + 1 : gate_count + 2, :]
    ranks = lax.broadcasted_iota(jnp.int32, (capacity, side.shape[1]), 0).astype(f32)
    hit = (ranks == slot) & (which == scenario.astype(f32))
    return hit.astype(f32).astype(bf16)


def prep_kernel(gate_count, tiled, pads, feats, sid, gate_rows, expand, pack, probs, pieces, scr):
    rows = feats.shape[0]
    scenarios = gate_rows.shape[0] // AUX
    x = feats[...]
    logits = mm(gate_rows[...], x, 1, 1)
    own = jnp.zeros((AUX, rows), f32)
    ids = sid[...]
    pad = jnp.zeros((1, rows), f32)
    for s in range(scenarios):
        hit = ids == s
        own = own + jnp.where(hit, logits[s * AUX : (s + 1) * AUX], 0.0)
        pad = pad + jnp.where(hit, pads[s].astype(f32), 0.0)
    labels = lax.broadcasted_iota(jnp.int32, (AUX, rows), 0)
    own = jnp.where(labels < gate_count, own, -jnp.inf)
    top = jnp.max(own, axis=0, keepdims=True)
    raised = jnp.exp(own - top)
    share = raised / jnp.sum(raised, axis=0, keepdims=True)
    probs[...] = share
    member = (ids == labels).astype(f32)
    earlier = (
        lax.broadcasted_iota(jnp.int32, (rows, rows), 0)
        < lax.broadcasted_iota(jnp.int32, (rows, rows), 1)
    ).astype(f32).astype(bf16)
    rank = jnp.sum(mm(member.astype(bf16), earlier) * member, axis=0, keepdims=True)
    slot = jnp.where(rank < pad, rank, -1.0)
    scr[...] = share
    scr[gate_count : gate_count + 1, :] = ids.astype(f32)
    scr[gate_count + 1 : gate_count + 2, :] = slot
    side = scr[...].astype(bf16)
    pack[:rows, :] = x
    pack[rows:, :rows] = side[: AUX // 2]
    pack[rows:, rows:] = side[AUX // 2 :]
    if tiled:
        chips, _, total = pieces.shape
        count = expand.shape[0]
        lanes = total // count
        for k in range(count):
            for chip in range(chips):
                pieces[chip, :, k * lanes : (k + 1) * lanes] = expand[
                    k, :, chip * lanes : (chip + 1) * lanes
                ]
    else:
        pieces[...] = expand[...]


def unpack_kernel(n, gate_count, capacity, depth, scal, *refs):
    pieces = refs[:n]
    xp, xpt, gates, sel_own, sel_other, x_own, x_other = refs[n:]
    m = pieces[0].shape[0]
    rows = pieces[0].shape[1] - AUX // 2
    width = xp.shape[1]
    turn = turn_matrix(width, depth, scal[3])
    tail = jnp.zeros((capacity, x_own.shape[1] - width - AUX), bf16)
    for k in range(n):
        for b in range(m):
            at = (k * m + b) * rows
            x = pieces[k][b, :rows, :]
            side = side_of(pieces[k][b, rows:, :])
            xp[at : at + rows, :] = mm(x, turn, 1, 1).astype(bf16)
            xpt[:, at : at + rows] = mm(turn, x, 1, 1).astype(bf16)
            gates[at : at + rows, :] = mm(side, eye(AUX), 0, 0).astype(bf16)
            spot = slice((k * m + b) * capacity, (k * m + b + 1) * capacity)
            for which, sel_out, out in ((0, sel_own, x_own), (1, sel_other, x_other)):
                sel = selector(side, gate_count, scal[which], capacity)
                sel_out[spot, :] = sel
                out[spot, :width] = mm(sel, x).astype(bf16)
                out[spot, width : width + AUX] = mm(sel, side, 1, 1).astype(bf16)
                out[spot, width + AUX :] = tail


def compact_kernel(n, sel_own, sel_other, *refs):
    values, outs = refs[:n], refs[n:]
    m = values[0].shape[0]
    capacity = outs[0].shape[0] // (n * m)
    for k in range(n):
        for b in range(m):
            spot = slice((k * m + b) * capacity, (k * m + b + 1) * capacity)
            for sel, out in zip((sel_own, sel_other), outs):
                out[spot, :] = mm(sel[spot, :], values[k][b]).astype(bf16)


def chosen_gate(x, width, column):
    gates = x[:, width:].astype(f32)
    lanes = lax.broadcasted_iota(jnp.int32, gates.shape, 1)
    return jnp.sum(jnp.where(lanes == column, gates, 0.0), axis=1, keepdims=True)


def hidden_lanes(j):
    return pl.ds(pl.multiple_of(j * TILE, TILE), TILE)


def scenario_forward_kernel(shared, span, scal, own, other, widen, narrow, out_own, out_other, gated):
    half, width = out_own.shape
    chunk = min(half, CHUNK)

    def tile(j, _):
        lanes = hidden_lanes(j)
        column = shared + scal[2] + (j * TILE) // span
        for base, source in ((0, own), (half, other)):
            for at in range(0, half, chunk):
                x = source[at : at + chunk, :]
                linear = mm(x[:, :width], widen[:, lanes])
                active = linear * sigmoid(linear)
                gate = chosen_gate(x, width, column)
                gated[base + at : base + at + chunk, lanes] = (gate * active).astype(bf16)
        return 0

    lax.fori_loop(0, widen.shape[1] // TILE, tile, 0)
    out_own[...] = mm(gated[:half, :], narrow[...]).astype(bf16)
    out_other[...] = mm(gated[half:, :], narrow[...]).astype(bf16)


def scenario_slope_kernel(
    shared, span, scal, own, other, widen, active_out, gated_turned, slope_out, turned
):
    half = own.shape[0]
    width = widen.shape[0]
    chunk = min(half, CHUNK)
    for base, source in ((0, own), (half, other)):
        for at in range(0, half, chunk):
            turned[:, base + at : base + at + chunk] = mm(
                eye(width), source[at : at + chunk, :width], 1, 1
            ).astype(bf16)

    def tile(j, _):
        lanes = hidden_lanes(j)
        column = shared + scal[2] + (j * TILE) // span
        for base, source in ((0, own), (half, other)):
            for at in range(0, half, chunk):
                x = source[at : at + chunk, :]
                gate = chosen_gate(x, width, column)
                linear = mm(x[:, :width], widen[:, lanes])
                sig = sigmoid(linear)
                active = linear * sig
                spot = slice(base + at, base + at + chunk)
                active_out[spot, lanes] = active.astype(bf16)
                slope_out[spot, lanes] = (gate * (sig + active * (1.0 - sig))).astype(bf16)
                gated_turned[lanes, spot] = jnp.transpose(gate * active).astype(bf16)
        return 0

    lax.fori_loop(0, widen.shape[1] // TILE, tile, 0)


def shared_forward_kernel(first, gate_rows, build, core, xp, gates, w1a, w1b, w2a, w2b, *refs):
    sel_own, sel_other, from_own, from_other = refs[:4]
    outs = refs[4:]
    gated = outs[-1]
    outs = outs[:-1]
    if build:
        w1, w2 = outs[-2:]
        outs = outs[:-2]
        half = w1a.shape[0]
        w1[:half, :] = w1a[...]
        w1[half:, :] = w1b[...]
        experts, part, _ = w2a.shape
        for k in range(experts):
            mine, theirs = w2a[k], w2b[k]
            low = jnp.where(core[3] == 0, mine, theirs)
            high = jnp.where(core[3] == 0, theirs, mine)
            w2[2 * k * part : (2 * k + 1) * part, :] = low
            w2[(2 * k + 1) * part : 2 * (k + 1) * part, :] = high
    else:
        w1, w2 = w1a, w2a
    m, rows, _ = outs[0].shape
    capacity = sel_own.shape[0] * rows // xp.shape[0]
    total = len(outs) * m * rows
    chunk = min(total, CHUNK)

    def tile(j, _):
        lanes = hidden_lanes(j)
        picks = spread(j, gate_rows)
        for at in range(0, total, chunk):
            spot = slice(first + at, first + at + chunk)
            linear = mm(xp[spot, :], w1[:, lanes])
            active = linear * sigmoid(linear)
            gated[at : at + chunk, lanes] = (mm(gates[spot, :], picks) * active).astype(bf16)
        return 0

    lax.fori_loop(0, w1.shape[1] // TILE, tile, 0)
    chunk = min(total, 512)
    for at in range(0, total, chunk):
        mixed = mm(gated[at : at + chunk, :], w2[...])
        for piece in range(at // rows, (at + chunk) // rows):
            start = (first // rows + piece) * capacity
            spot = slice(start, start + capacity)
            extra = mm(sel_own[spot, :], from_own[spot, :], 0, 0)
            extra += mm(sel_other[spot, :], from_other[spot, :], 0, 0)
            value = mixed[piece * rows - at : (piece + 1) * rows - at] + extra
            outs[piece // m][piece % m] = value.astype(bf16)


def shared_slope_kernel(gate_rows, xp, gates, w1, active_out, gated_turned, slope_out):
    total = xp.shape[0]
    chunk = min(total, CHUNK)

    def tile(j, _):
        lanes = hidden_lanes(j)
        picks = spread(j, gate_rows)
        for at in range(0, total, chunk):
            spot = slice(at, at + chunk)
            linear = mm(xp[spot, :], w1[:, lanes])
            sig = sigmoid(linear)
            active = linear * sig
            gate = mm(gates[spot, :], picks)
            active_out[spot, lanes] = active.astype(bf16)
            slope_out[spot, lanes] = (gate * (sig + active * (1.0 - sig))).astype(bf16)
            gated_turned[lanes, spot] = jnp.transpose(gate * active).astype(bf16)
        return 0

    lax.fori_loop(0, w1.shape[1] // TILE, tile, 0)


def softmax(v):
    raised = jnp.exp(v - jnp.max(v, axis=1, keepdims=True))
    return raised / jnp.sum(raised, axis=1, keepdims=True)


def head_kernel(count, *refs):
    parts = refs[:count]
    head, mentor, grad, head_part = refs[count:]
    layer = parts[0][...].astype(f32)
    for part in parts[1:]:
        layer = layer + part[...].astype(f32)
    rounded = layer.astype(bf16)
    student = mm(rounded, head[...])
    value = (2.0 * (softmax(student * 0.5) - softmax(mentor[...] * 0.5))).astype(bf16)
    grad[...] = value
    head_part[...] = mm(rounded, value, 0, 0)


def shared_backward_kernel(n, gate_rows, depth, scal, *refs):
    logits = refs[:n]
    head, xpt, active, slope, w1, w2 = refs[n : n + 6]
    dx, mix, keep, sent, os, linear_grad = refs[n + 6 :]
    m, rows, _ = logits[0].shape
    for k in range(n):
        for b in range(m):
            at = (k * m + b) * rows
            os[at : at + rows, :] = mm(logits[k][b], head[...], 1, 1).astype(bf16)
    total = n * m * rows
    chunk = min(total, 2 * CHUNK)
    half = keep.shape[0]
    mix[...] = jnp.zeros_like(mix)

    def tile(j, _):
        lanes = hidden_lanes(j)
        picks = spread(j, gate_rows)
        for at in range(0, total, chunk):
            spot = slice(at, at + chunk)
            hidden = mm(os[spot, :], w2[lanes, :], 1, 1)
            linear_grad[spot, lanes] = (hidden * slope[spot, lanes].astype(f32)).astype(bf16)
            product = (hidden * active[spot, lanes].astype(f32)).astype(bf16)
            mix[spot, :] += mm(product, picks, 1, 1)
        first = mm(xpt[...], linear_grad[:, lanes])
        keep[:, lanes] = first[:half]
        sent[:, lanes] = first[half:].astype(bf16)
        return 0

    lax.fori_loop(0, w1.shape[1] // TILE, tile, 0)
    turn = turn_matrix(w1.shape[0], depth, scal[3])
    chunk = min(total, 1024)
    for at in range(0, total, chunk):
        spot = slice(at, at + chunk)
        value = mm(linear_grad[spot, :], w1[...], 1, 1).astype(bf16)
        dx[spot, :] = mm(value, turn).astype(bf16)


def reduce_grad_kernel(gate_rows, scal, gated_turned, os, keep, sent):
    part = keep.shape[1]

    def tile(j, _):
        value = mm(gated_turned[hidden_lanes(j), :], os[...])
        for e in range(TILE // gate_rows):
            low = value[e * gate_rows : e * gate_rows + part]
            high = value[e * gate_rows + part : (e + 1) * gate_rows]
            k = j * (TILE // gate_rows) + e
            keep[k] = jnp.where(scal[3] == 0, low, high)
            sent[k] = jnp.where(scal[3] == 0, high, low).astype(bf16)
        return 0

    lax.fori_loop(0, gated_turned.shape[0] // TILE, tile, 0)


def scenario_backward_kernel(
    shared, span, scal, logit_own, logit_other, head, widen, narrow, active, slope,
    out_own, out_other, os, linear_grad, mix,
):
    half = out_own.shape[0]
    width = narrow.shape[1]
    os[:half, :] = mm(logit_own[...], head[...], 1, 1).astype(bf16)
    os[half:, :] = mm(logit_other[...], head[...], 1, 1).astype(bf16)
    mix[...] = jnp.zeros_like(mix)
    chunk = min(2 * half, 2 * CHUNK)

    def tile(j, _):
        lanes = hidden_lanes(j)
        column = shared + scal[2] + (j * TILE) // span
        picks = (
            lax.broadcasted_iota(jnp.int32, (TILE, mix.shape[1]), 1) == column
        ).astype(f32).astype(bf16)
        for at in range(0, 2 * half, chunk):
            spot = slice(at, at + chunk)
            hidden = mm(os[spot, :], narrow[lanes, :], 1, 1)
            linear_grad[spot, lanes] = (hidden * slope[spot, lanes].astype(f32)).astype(bf16)
            product = (hidden * active[spot, lanes].astype(f32)).astype(bf16)
            mix[spot, :] += mm(product, picks)
        return 0

    lax.fori_loop(0, widen.shape[1] // TILE, tile, 0)
    for at, out in ((0, out_own), (half, out_other)):
        out[:, :width] = mm(linear_grad[at : at + half, :], widen[...], 1, 1).astype(bf16)
        out[:, width:] = mix[at : at + half, :].astype(bf16)


def scenario_weight_kernel(turned, linear_grad, gated_turned, os, dwiden, dnarrow):
    def tile(j, _):
        lanes = hidden_lanes(j)
        dwiden[:, lanes] = mm(turned[...], linear_grad[:, lanes])
        dnarrow[lanes, :] = mm(gated_turned[lanes, :], os[...])
        return 0

    lax.fori_loop(0, dwiden.shape[1] // TILE, tile, 0)


def scatter_kernel(n, gate_count, *refs):
    pieces = refs[:n]
    sel_own, sel_other, gates, dx, mix, from_own, from_other = refs[n : n + 7]
    outs, gate_part, wide = refs[n + 7 : -2], refs[-2], refs[-1]
    m, packed, width = outs[0].shape
    rows = packed - AUX // 2
    capacity = sel_own.shape[0] // (n * m)
    live = lax.broadcasted_iota(jnp.int32, (rows, AUX), 1) < gate_count
    total = jnp.zeros(gate_part.shape, f32)
    for k in range(n):
        for b in range(m):
            piece = k * m + b
            slots = slice(piece * capacity, (piece + 1) * capacity)
            extra = mm(sel_own[slots, :], from_own[slots, :], 0, 0)
            extra += mm(sel_other[slots, :], from_other[slots, :], 0, 0)
            spot = slice(piece * rows, (piece + 1) * rows)
            outs[k][b, :rows, :] = (dx[spot, :].astype(f32) + extra[:, :width]).astype(bf16)
            dots = mix[spot, :] + extra[:, width : width + AUX]
            turned = mm(eye(AUX), dots.astype(bf16), 1, 1).astype(bf16)
            outs[k][b, rows:, :rows] = turned[: AUX // 2]
            outs[k][b, rows:, rows:] = turned[AUX // 2 :]
            share = jnp.where(live, gates[spot, :].astype(f32), 0.0)
            share = share / jnp.sum(share, axis=1, keepdims=True)
            score = share * (dots - jnp.sum(share * dots, axis=1, keepdims=True))
            score = mm(eye(AUX), score.astype(bf16), 1, 1)
            ids = side_of(pieces[k][b, rows:, :])[gate_count : gate_count + 1, :].astype(f32)
            for s in range(gate_part.shape[0] // AUX):
                wide[s * AUX : (s + 1) * AUX, :] = jnp.where(ids == s, score, 0.0).astype(bf16)
            total = total + mm(wide[...], pieces[k][b, :rows, :])
    gate_part[...] = total


def final_kernel(count, gate_count, *refs):
    parts = refs[:count]
    feats, sid, probs, gate_rows, out, wide = refs[count:]
    rows = feats.shape[0]
    total = parts[0][...].astype(f32)
    for part in parts[1:]:
        total = total + part[...].astype(f32)
    tail = total[rows:]
    half = tail.shape[1] // 2
    dots = jnp.concatenate([tail[:, :half], tail[:, half:]], axis=0)
    share = probs[...]
    live = lax.broadcasted_iota(jnp.int32, (AUX, rows), 0) < gate_count
    dots = jnp.where(live, dots, 0.0)
    score = share * (dots - jnp.sum(share * dots, axis=0, keepdims=True))
    score = score.astype(bf16).astype(f32)
    ids = sid[...]
    for s in range(gate_rows.shape[0] // AUX):
        wide[s * AUX : (s + 1) * AUX, :] = jnp.where(ids == s, score, 0.0).astype(bf16)
    out[...] = (total[:rows] + mm(wide[...], gate_rows[...], 0, 0)).astype(bf16)


def expand_grad_kernel(pieces, out):
    count, _, hidden = out.shape
    chips = pieces.shape[0]
    lanes = hidden // chips
    for k in range(count):
        for chip in range(chips):
            out[k, :, chip * lanes : (chip + 1) * lanes] = pieces[
                chip, :, k * lanes : (k + 1) * lanes
            ].astype(f32)


def body(
    features,
    scenario_id,
    scenario_pads,
    device_slot,
    mentor,
    gate_weight,
    expand,
    reduce,
    scenario_widen,
    scenario_narrow,
    head,
):
    rows, width = features.shape
    devices = lax.axis_size(AXIS)
    index = lax.axis_index(AXIS)
    core = index % 2
    chips = devices // 2
    near = 2 ** ((chips.bit_length() - 1) // 2)
    far = chips // near
    flat = chips <= 8
    n, m = (chips, 1) if flat else (near, far)
    shared, depth, hidden = expand.shape
    lanes = hidden // chips
    scenarios, _, gates = gate_weight.shape
    capacity = rows // 4
    group = devices // scenarios
    slot_width = scenario_widen.shape[2]
    span = min(hidden, slot_width)
    classes = head.shape[1]
    all_rows = chips * rows
    slots = chips * capacity
    hidden_chip = shared * lanes
    groups = [[2 * r + c for r in range(chips)] for c in range(2)]

    def send(value, mask):
        return lax.ppermute(value, AXIS, [(i, i ^ mask) for i in range(devices)])

    def gather(value):
        column = [value] + [send(value, 2 * near * b) for b in range(1, far)]
        if flat:
            out = [v[None] for v in column]
            for a in range(1, near):
                out += [send(v, 2 * a)[None] for v in column]
            return out
        stacked = jnp.stack(column)
        return [stacked] + [send(stacked, 2 * a) for a in range(1, near)]

    def scatter(home, away):
        if flat:
            column = []
            for b in range(far):
                total = home[b][0].astype(f32)
                for a in range(1, near):
                    total = total + send(away[(a - 1) * far + b][0], 2 * a).astype(f32)
                column.append(total if b == 0 else total.astype(bf16))
        else:
            total = home[0].astype(f32)
            for a in range(1, near):
                total = total + send(away[a - 1], 2 * a).astype(f32)
            column = [total[0]] + [total[b].astype(bf16) for b in range(1, far)]
        return [column[0]] + [send(column[b], 2 * near * b) for b in range(1, far)]

    def total_of(value):
        value = value + send(value, 1)
        mask = 2
        while mask < devices:
            half = value.astype(bf16)
            value = half.astype(f32) + send(half, mask).astype(f32)
            mask *= 2
        return value

    own_slot = lax.dynamic_index_in_dim(device_slot, index, keepdims=False)
    other_slot = lax.dynamic_index_in_dim(device_slot, index ^ 1, keepdims=False)
    first_expert = own_slot % group * slot_width // hidden
    scal = jnp.stack([own_slot // group, other_slot // group, first_expert, core]).astype(jnp.int32)
    sid = scenario_id.reshape(1, rows)
    gate_rows = jnp.pad(
        jnp.transpose(gate_weight, (0, 2, 1)), ((0, 0), (0, AUX - gates), (0, 0))
    ).reshape(scenarios * AUX, width)
    widen, narrow = scenario_widen[0], scenario_narrow[0]
    tiled = lanes % 128 == 0 and depth % 16 == 0
    if not tiled:
        expand = expand.reshape(shared, depth, chips, lanes).transpose(2, 1, 0, 3)
        expand = expand.reshape(chips, depth, hidden_chip)

    pack_rows = rows + AUX // 2
    pack, probs, pieces = call(
        functools.partial(prep_kernel, gates, tiled),
        [
            struct((pack_rows, width), bf16),
            struct((AUX, rows), f32),
            struct((chips, depth, hidden_chip), bf16),
        ],
        [scenario_pads, features, sid, gate_rows, expand],
        [SCALARS] + [None] * 4,
        [pltpu.VMEM((AUX, rows), f32)],
        flops=10**9,
        limit=16,
    )
    w2a = reduce
    w2b = send(reduce, 1)
    w1a = lax.all_to_all(
        pieces, AXIS, split_axis=0, concat_axis=0, tiled=True, axis_index_groups=groups
    ).reshape(width // 2, hidden_chip)
    w1b = send(w1a, 1)

    got = gather(pack)
    xp, xpt, gate_columns, sel_own, sel_other, x_own, x_send = call(
        functools.partial(unpack_kernel, n, gates, capacity, depth),
        [
            struct((all_rows, width), bf16),
            struct((width, all_rows), bf16),
            struct((all_rows, AUX), bf16),
            struct((slots, rows), bf16),
            struct((slots, rows), bf16),
            struct((slots, width + 128), bf16),
            struct((slots, width + 128), bf16),
        ],
        [scal, *got],
        [SCALARS] + [None] * n,
        flops=2 * 10**9,
        limit=SMALL,
    )
    x_other = send(x_send, 1)
    out_own, out_send = call(
        functools.partial(scenario_forward_kernel, shared, span),
        [struct((slots, width), bf16)] * 2,
        [scal, x_own, x_other, widen, narrow],
        [SCALARS] + [None] * 4,
        [pltpu.VMEM((2 * slots, slot_width), bf16)],
        flops=3 * 10**9,
        limit=SMALL,
    )
    out_other = send(out_send, 1)
    mixing = [sel_own, sel_other, out_own, out_other]
    home_rows = far * rows
    *away, w1, w2 = call(
        functools.partial(shared_forward_kernel, home_rows, lanes, True),
        [struct((m, rows, width), bf16)] * (n - n // near)
        + [struct((width, hidden_chip), bf16), struct((hidden_chip, width), bf16)],
        [scal, xp, gate_columns, w1a, w1b, w2a, w2b, *mixing],
        [SCALARS] + [None] * 10,
        [pltpu.VMEM((all_rows - home_rows, hidden_chip), bf16)],
        flops=3 * 10**9,
        limit=SMALL,
    )
    home = call(
        functools.partial(shared_forward_kernel, 0, lanes, False),
        [struct((m, rows, width), bf16)] * (n // near),
        [scal, xp, gate_columns, w1, w1, w2, w2, *mixing],
        [SCALARS] + [None] * 10,
        [pltpu.VMEM((home_rows, hidden_chip), bf16)],
        flops=3 * 10**9,
        limit=SMALL,
    )
    layer_parts = scatter(home, away)
    active, gated_turned, slope = call(
        functools.partial(shared_slope_kernel, lanes),
        [
            struct((all_rows, hidden_chip), bf16),
            struct((hidden_chip, all_rows), bf16),
            struct((all_rows, hidden_chip), bf16),
        ],
        [xp, gate_columns, w1],
        flops=6 * 10**9,
        limit=BIG,
    )
    scen_active, scen_gated, scen_slope, x_turned = call(
        functools.partial(scenario_slope_kernel, shared, span),
        [
            struct((2 * slots, slot_width), bf16),
            struct((slot_width, 2 * slots), bf16),
            struct((2 * slots, slot_width), bf16),
            struct((width, 2 * slots), bf16),
        ],
        [scal, x_own, x_other, widen],
        [SCALARS] + [None] * 3,
        flops=4 * 10**9,
        limit=BIG,
    )
    logit_grad, head_part = call(
        functools.partial(head_kernel, len(layer_parts)),
        [struct((rows, classes), bf16), struct((width, classes), f32)],
        [*layer_parts, head, mentor],
        flops=10**9,
        limit=8,
    )
    logits = gather(logit_grad)
    head_total = total_of(head_part)

    l_own, l_send = call(
        functools.partial(compact_kernel, n),
        [struct((slots, classes), bf16)] * 2,
        [sel_own, sel_other, *logits],
        flops=10**9,
        limit=SMALL,
    )
    l_other = send(l_send, 1)
    dx, mix, dw1_keep, dw1_send, os, _ = call(
        functools.partial(shared_backward_kernel, n, lanes, depth),
        [
            struct((all_rows, width), bf16),
            struct((all_rows, AUX), f32),
            struct((width // 2, hidden_chip), f32),
            struct((width // 2, hidden_chip), bf16),
            struct((all_rows, width), bf16),
            struct((all_rows, hidden_chip), bf16),
        ],
        [scal, *logits, head, xpt, active, slope, w1, w2],
        [SCALARS] + [None] * (n + 6),
        flops=5 * 10**9,
        limit=BIG,
    )
    dw1 = (dw1_keep + send(dw1_send, 1).astype(f32)).astype(bf16)
    dw1 = lax.all_to_all(
        dw1.reshape(chips, depth, hidden_chip),
        AXIS, split_axis=0, concat_axis=0, tiled=True, axis_index_groups=groups,
    )
    if tiled:
        (expand_grad,) = call(
            expand_grad_kernel, [struct((shared, depth, hidden), f32)], [dw1], limit=8
        )
    else:
        expand_grad = dw1.reshape(chips, depth, shared, lanes).transpose(2, 1, 0, 3)
        expand_grad = expand_grad.reshape(shared, depth, hidden).astype(f32)

    dx_own, dx_send, scen_os, scen_grad = call(
        functools.partial(scenario_backward_kernel, shared, span),
        [struct((slots, width + 128), bf16)] * 2
        + [struct((2 * slots, width), bf16), struct((2 * slots, slot_width), bf16)],
        [scal, l_own, l_other, head, widen, narrow, scen_active, scen_slope],
        [SCALARS] + [None] * 7,
        [pltpu.VMEM((2 * slots, 128), f32)],
        flops=2 * 10**9,
        limit=BIG,
    )
    dx_other = send(dx_send, 1)
    *grad_parts, gate_part = call(
        functools.partial(scatter_kernel, n, gates),
        [struct((m, pack_rows, width), bf16)] * n + [struct((scenarios * AUX, width), f32)],
        [*got, sel_own, sel_other, gate_columns, dx, mix, dx_own, dx_other],
        None,
        [pltpu.VMEM((scenarios * AUX, rows), bf16)],
        flops=2 * 10**9,
        limit=SMALL,
    )
    grad_parts = scatter(grad_parts[: n // near], grad_parts[n // near :])
    gate_part = gate_part.reshape(scenarios, AUX, width)[:, :gates]
    gate_total = jnp.transpose(total_of(gate_part), (0, 2, 1))
    dw2_keep, dw2_send = call(
        functools.partial(reduce_grad_kernel, lanes),
        [struct((shared, lanes // 2, width), f32), struct((shared, lanes // 2, width), bf16)],
        [scal, gated_turned, os],
        [SCALARS] + [None] * 2,
        flops=2 * 10**9,
        limit=BIG,
    )
    reduce_grad = dw2_keep + send(dw2_send, 1).astype(f32)
    widen_grad, narrow_grad = call(
        scenario_weight_kernel,
        [struct((width, slot_width), f32), struct((slot_width, width), f32)],
        [x_turned, scen_grad, scen_gated, scen_os],
        flops=3 * 10**9,
        limit=BIG,
    )
    (feature_grad,) = call(
        functools.partial(final_kernel, len(grad_parts), gates),
        [struct((rows, width), bf16)],
        [*grad_parts, features, sid, probs, gate_rows],
        None,
        [pltpu.VMEM((scenarios * AUX, rows), bf16)],
        flops=10**9,
        limit=8,
    )
    return (
        feature_grad,
        expand_grad,
        reduce_grad,
        widen_grad[None],
        narrow_grad[None],
        gate_total,
        head_total,
    )


def solution(mesh):
    placed = (
        P(("groups", "expert"), None),
        P(("groups", "expert")),
        P("groups"),
        P(),
        P(("groups", "expert"), None),
        P(),
        P(None, "expert", None),
        P(None, "expert", None),
        P("expert", None, None),
        P("expert", None, None),
        P(),
    )
    return jax.shard_map(
        body,
        mesh=mesh,
        in_specs=placed,
        out_specs=(
            P(("groups", "expert"), None),
            P("groups", "expert", None),
            P("groups", "expert", None),
            P(("groups", "expert"), None, None),
            P(("groups", "expert"), None, None),
            P("groups", None, None),
            P("groups", None),
        ),
        check_vma=False,
    )
```

```python
import functools

import jax
import jax.numpy as jnp
from jax import lax
from jax.experimental import pallas as pl
from jax.experimental.pallas import tpu as pltpu
from jax.sharding import PartitionSpec as P

AXIS = "expert"
TILE = 512
AUX = 32
bf16 = jnp.bfloat16
f32 = jnp.float32
CHUNK = 512
FIRST, SMALL, BIG = 60, 16, 32
COST = 100000


def mm(left, right, left_dim=1, right_dim=0):
    return lax.dot_general(
        left, right, (((left_dim,), (right_dim,)), ((), ())), preferred_element_type=f32
    )


def call(kernel, out_shapes, operands, in_specs=None, scratch=(), limit=48):
    specs = in_specs or [None] * len(operands)
    specs = [pl.BlockSpec(memory_space=pltpu.VMEM) if s is None else s for s in specs]
    return pl.pallas_call(
        kernel,
        out_shape=out_shapes,
        in_specs=specs,
        out_specs=[pl.BlockSpec(memory_space=pltpu.VMEM) for _ in out_shapes],
        scratch_shapes=list(scratch),
        compiler_params=pltpu.CompilerParams(vmem_limit_bytes=limit * 1024 * 1024),
        cost_estimate=pl.CostEstimate(flops=COST, bytes_accessed=COST, transcendentals=0),
    )(*operands)


SCALARS = pl.BlockSpec(memory_space=pltpu.SMEM)


def own_core():
    return lax.rem(lax.axis_index(AXIS), 2)


def struct(shape, kind):
    return jax.ShapeDtypeStruct(shape, kind)


def sigmoid(v):
    return 0.5 * (1.0 + jnp.tanh(0.5 * v))


def eye(size):
    rows = lax.broadcasted_iota(jnp.int32, (size, size), 0)
    cols = lax.broadcasted_iota(jnp.int32, (size, size), 1)
    return (rows == cols).astype(f32).astype(bf16)


def spread(tile, size, expert_lanes):
    rows = lax.broadcasted_iota(jnp.int32, (AUX, size), 0)
    lanes = lax.broadcasted_iota(jnp.int32, (AUX, size), 1) + tile * size
    first = rows * expert_lanes
    return ((lanes >= first) & (lanes < first + expert_lanes)).astype(f32).astype(bf16)


def turn_matrix(size, depth, core):
    place = lax.broadcasted_iota(jnp.int32, (size, size), 0)
    column = lax.broadcasted_iota(jnp.int32, (size, size), 1)
    half = size // 2
    other = place // half
    place = place - other * half
    chip = place // depth
    which = jnp.where(core == 0, other, 1 - other)
    return (column == (chip * 2 + which) * depth + (place - chip * depth)).astype(f32).astype(bf16)


def side_of(piece):
    half = piece.shape[1] // 2
    return jnp.concatenate([piece[:, :half], piece[:, half:]], axis=0)


def selector(side, gate_count, owner, capacity):
    wide = side.astype(f32)
    which = wide[gate_count : gate_count + 1, :]
    slot = wide[gate_count + 1 : gate_count + 2, :]
    ranks = lax.broadcasted_iota(jnp.int32, (capacity, side.shape[1]), 0).astype(f32)
    hit = (ranks == slot) & (which == owner)
    return hit.astype(f32).astype(bf16)


def placement(own_side, gate_count):
    wide = own_side.astype(f32)
    rows = [wide[gate_count + 2 + i : gate_count + 3 + i, :] for i in range(4)]
    return (rows[0], rows[1]), (rows[2], rows[3])


def gate_picks(first):
    shape = (AUX, first.shape[1])
    rows = lax.broadcasted_iota(jnp.int32, shape, 0)
    lanes = lax.broadcasted_iota(jnp.int32, shape, 1)
    return ((rows - lanes).astype(f32) == first).astype(f32).astype(bf16)


def by_scenario(ids, scenarios):
    labels = lax.broadcasted_iota(jnp.int32, (scenarios, ids.shape[1]), 0)
    return (labels == ids).astype(f32)[None]


def prep_kernel(shared, hidden, slot_width, pads, slots, feats, sid, gate, pack, probs, scr):
    scenarios = pads.shape[0]
    gate_count = gate.shape[0] // scenarios
    rows = feats.shape[0]
    x = feats[...]
    ids = sid[...]
    scr[...] = jnp.zeros_like(scr)
    pad = jnp.zeros((1, rows), f32)
    for s in range(scenarios):
        pad = pad + jnp.where(ids == s, pads[s].astype(f32), 0.0)
    logits = mm(gate[...], x, 1, 1).reshape(gate_count, scenarios, rows)
    own = jnp.sum(logits * by_scenario(ids, scenarios), axis=1)
    top = jnp.max(own, axis=0, keepdims=True)
    raised = jnp.exp(own - top)
    scr[:gate_count, :] = raised / jnp.sum(raised, axis=0, keepdims=True)
    probs[...] = scr[...]
    labels = lax.broadcasted_iota(jnp.int32, (AUX, rows), 0)
    member = (ids == labels).astype(f32)
    earlier = (
        lax.broadcasted_iota(jnp.int32, (rows, rows), 0)
        < lax.broadcasted_iota(jnp.int32, (rows, rows), 1)
    ).astype(f32).astype(bf16)
    rank = jnp.sum(mm(member.astype(bf16), earlier) * member, axis=0, keepdims=True)
    slot = jnp.where(rank < pad, rank, -1.0)
    scr[gate_count : gate_count + 1, :] = ids.astype(f32)
    scr[gate_count + 1 : gate_count + 2, :] = slot
    index = lax.axis_index(AXIS)
    group = slots.shape[0] // scenarios
    for i, device in enumerate((index, index + 1 - 2 * lax.rem(index, 2))):
        owned = slots[device]
        first = shared + lax.rem(owned, group) * slot_width // hidden
        for j, value in enumerate((owned // group, first)):
            at = gate_count + 2 + 2 * i + j
            scr[at : at + 1, :] = jnp.zeros((1, rows), f32) + value.astype(f32)
    side = scr[...].astype(bf16)
    pack[:rows, :] = x
    pack[rows:, :rows] = side[: AUX // 2]
    pack[rows:, rows:] = side[AUX // 2 :]


def tile_kernel(tiled, expand, pieces):
    if tiled:
        chips, _, total = pieces.shape
        count = expand.shape[0]
        lanes = total // count
        for k in range(count):
            for chip in range(chips):
                pieces[chip, :, k * lanes : (k + 1) * lanes] = expand[
                    k, :, chip * lanes : (chip + 1) * lanes
                ]
    else:
        pieces[...] = expand[...]


def own_place(pieces, gate_count):
    return placement(side_of(pieces[0][0, pieces[0].shape[1] - AUX // 2 :, :]), gate_count)


def compact_kernel(n, gate_count, capacity, *refs):
    pieces, logits, outs = refs[:n], refs[n:-2], refs[-2:]
    m = pieces[0].shape[0]
    rows = pieces[0].shape[1] - AUX // 2
    width = pieces[0].shape[2]
    places = own_place(pieces, gate_count)
    for k in range(n):
        for b in range(m):
            x = pieces[k][b, :rows, :]
            side = side_of(pieces[k][b, rows:, :])
            spot = slice((k * m + b) * capacity, (k * m + b + 1) * capacity)
            for (owner, first), out in zip(places, outs):
                sel = selector(side, gate_count, owner, capacity)
                out[spot, :width] = mm(sel, x).astype(bf16)
                gates = mm(sel, side, 1, 1).astype(bf16)
                out[spot, width : width + rows] = mm(gates, gate_picks(first)).astype(bf16)
                if logits:
                    out[spot, width + rows :] = mm(sel, logits[k][b]).astype(bf16)


def chosen_gate(x, width, expert):
    gates = x[:, width : width + 128].astype(f32)
    lanes = lax.broadcasted_iota(jnp.int32, gates.shape, 1)
    return jnp.sum(jnp.where(lanes == expert, gates, 0.0), axis=1, keepdims=True)


def hidden_lanes(j, size):
    return pl.ds(pl.multiple_of(j * size, size), size)


def scenario_forward_kernel(hidden, own, other, widen, narrow, out_own, out_other, gated):
    half, width = out_own.shape
    total = widen.shape[1]
    size, chunk = min(TILE, total), min(half, CHUNK)

    def tile(j, _):
        lanes = hidden_lanes(j, size)
        for base, source in ((0, own), (half, other)):
            for at in range(0, half, chunk):
                x = source[at : at + chunk, :]
                gate = chosen_gate(x, width, (j * size) // hidden)
                linear = mm(x[:, :width], widen[:, lanes])
                spot = slice(base + at, base + at + chunk)
                gated[spot, lanes] = (gate * (linear * sigmoid(linear))).astype(bf16)
        return 0

    lax.fori_loop(0, total // size, tile, 0)
    out_own[...] = mm(gated[:half, :], narrow[...]).astype(bf16)
    out_other[...] = mm(gated[half:, :], narrow[...]).astype(bf16)


def unpack(pieces, turn, xs, gates, xt=None):
    m, packed, _ = pieces[0].shape
    rows = packed - AUX // 2
    for k in range(len(pieces)):
        for b in range(m):
            spot = slice((k * m + b) * rows, (k * m + b + 1) * rows)
            x = pieces[k][b, :rows, :]
            xs[spot, :] = mm(x, turn, 1, 1).astype(bf16)
            gates[spot, :] = mm(side_of(pieces[k][b, rows:, :]), eye(AUX), 0, 0).astype(bf16)
            if xt is not None:
                xt[:, spot] = mm(turn, x, 1, 1).astype(bf16)


def join_weights(w1a, w1b, w2a, w2b, w1, w2):
    half = w1a.shape[0]
    w1[:half, :] = w1a[...]
    w1[half:, :] = w1b[...]
    experts, part, _ = w2a.shape
    core = own_core()
    for k in range(experts):
        mine, theirs = w2a[k], w2b[k]
        w2[2 * k * part : (2 * k + 1) * part, :] = jnp.where(core == 0, mine, theirs)
        w2[(2 * k + 1) * part : 2 * (k + 1) * part, :] = jnp.where(core == 0, theirs, mine)


def shared_forward_kernel(n, start, gate_rows, gate_count, depth, *refs):
    own, pieces = refs[0], refs[1 : n + 1]
    w1a, w1b, w2a, w2b, from_own, from_other, out, xs, gates, w1, w2, gated = refs[n + 1 :]
    join_weights(w1a, w1b, w2a, w2b, w1, w2)
    unpack(pieces, turn_matrix(w1.shape[0], depth, own_core()), xs, gates)
    count, rows, _ = out.shape
    m = pieces[0].shape[0]
    capacity = from_own.shape[0] // (w1.shape[0] // (2 * depth))
    places = own_place([own], gate_count)
    total = count * rows
    size, chunk = min(TILE, w1.shape[1]), min(total, CHUNK)

    def tile(j, _):
        lanes = hidden_lanes(j, size)
        picks = spread(j, size, gate_rows)
        for at in range(0, total, chunk):
            spot = slice(at, at + chunk)
            linear = mm(xs[spot, :], w1[:, lanes])
            active = linear * sigmoid(linear)
            gated[spot, lanes] = (mm(gates[spot, :], picks) * active).astype(bf16)
        return 0

    lax.fori_loop(0, w1.shape[1] // size, tile, 0)
    for at in range(0, total, chunk):
        mixed = mm(gated[at : at + chunk, :], w2[...])
        for piece in range(at // rows, (at + chunk) // rows):
            side = side_of(pieces[piece // m][piece % m, rows:, :])
            spot = slice((start + piece) * capacity, (start + piece + 1) * capacity)
            value = mixed[piece * rows - at : (piece + 1) * rows - at]
            for (owner, _), source in zip(places, (from_own, from_other)):
                value += mm(selector(side, gate_count, owner, capacity), source[spot, :], 0, 0)
            out[piece] = value.astype(bf16)


def softmax(v):
    raised = jnp.exp(v - jnp.max(v, axis=1, keepdims=True))
    return raised / jnp.sum(raised, axis=1, keepdims=True)


def head_kernel(count, *refs):
    parts = refs[:count]
    head, mentor, grad, head_part = refs[count:]
    layer = parts[0][...].astype(f32)
    for part in parts[1:]:
        layer = layer + part[...].astype(f32)
    rounded = layer.astype(bf16)
    student = mm(rounded, head[...])
    value = (2.0 * (softmax(student * 0.5) - softmax(mentor[...] * 0.5))).astype(bf16)
    grad[...] = value
    head_part[...] = mm(rounded, value, 0, 0)


def shared_backward_kernel(n, gate_rows, depth, *refs):
    pieces, logits = refs[:n], refs[n : 2 * n]
    head, w1a, w1b, w2a, w2b = refs[2 * n : 2 * n + 5]
    dx, mix, keep, sent, keep2, sent2 = refs[2 * n + 5 : 2 * n + 11]
    xp, xpt, gates, w1, w2, os, linear_grad, weighed = refs[2 * n + 11 :]
    core = own_core()
    turn = turn_matrix(w1.shape[0], depth, core)
    join_weights(w1a, w1b, w2a, w2b, w1, w2)
    unpack(pieces, turn, xp, gates, xpt)
    m, rows, _ = logits[0].shape
    for k in range(n):
        for b in range(m):
            at = (k * m + b) * rows
            os[at : at + rows, :] = mm(logits[k][b], head[...], 1, 1).astype(bf16)
    total = n * m * rows
    size, chunk = min(TILE, w1.shape[1]), min(total, CHUNK)
    half, part = keep.shape[0], keep2.shape[1]
    mix[...] = jnp.zeros_like(mix)

    def tile(j, _):
        lanes = hidden_lanes(j, size)
        picks = spread(j, size, gate_rows)
        for at in range(0, total, chunk):
            spot = slice(at, at + chunk)
            linear = mm(xp[spot, :], w1[:, lanes])
            hidden = mm(os[spot, :], w2[lanes, :], 1, 1)
            gate = mm(gates[spot, :], picks)
            sig = sigmoid(linear)
            active = linear * sig
            mix[spot, :] += mm((hidden * active).astype(bf16), picks, 1, 1)
            slope = sig + active * (1.0 - sig)
            linear_grad[spot, lanes] = (gate * hidden * slope).astype(bf16)
            weighed[spot, :] = (gate * active).astype(bf16)
        first = mm(xpt[...], linear_grad[:, lanes])
        keep[:, lanes] = first[:half].astype(keep.dtype)
        sent[:, lanes] = first[half:].astype(bf16)
        second = mm(weighed[...], os[...], 0, 0)
        for e in range(size // gate_rows):
            low = second[e * gate_rows : e * gate_rows + part]
            high = second[e * gate_rows + part : (e + 1) * gate_rows]
            k = j * (size // gate_rows) + e
            keep2[k] = jnp.where(core == 0, low, high)
            sent2[k] = jnp.where(core == 0, high, low).astype(bf16)
        return 0

    lax.fori_loop(0, w1.shape[1] // size, tile, 0)
    chunk = min(total, 1024)
    for at in range(0, total, chunk):
        spot = slice(at, at + chunk)
        value = mm(linear_grad[spot, :], w1[...], 1, 1).astype(bf16)
        dx[spot, :] = mm(value, turn).astype(bf16)


def scenario_backward_kernel(
    hidden_units, own, other, head, widen, narrow,
    out_own, out_other, dwiden, dnarrow, xs, xt, os, linear_grad, weighed, mix,
):
    half = out_own.shape[0]
    width = narrow.shape[1]
    total = widen.shape[1]
    xs[:half, :] = own[...]
    xs[half:, :] = other[...]
    os[...] = mm(xs[:, width + 128 :], head[...], 1, 1).astype(bf16)
    mix[...] = jnp.zeros_like(mix)
    size, chunk = min(TILE, total), min(2 * half, CHUNK)
    for at in range(0, 2 * half, chunk):
        xt[:, at : at + chunk] = mm(eye(width), xs[at : at + chunk, :width], 1, 1).astype(bf16)

    def tile(j, _):
        lanes = hidden_lanes(j, size)
        column = (j * size) // hidden_units
        picks = (
            lax.broadcasted_iota(jnp.int32, (size, mix.shape[1]), 1) == column
        ).astype(f32).astype(bf16)
        for at in range(0, 2 * half, chunk):
            spot = slice(at, at + chunk)
            x = xs[spot, :]
            gate = chosen_gate(x, width, column)
            linear = mm(x[:, :width], widen[:, lanes])
            hidden = mm(os[spot, :], narrow[lanes, :], 1, 1)
            sig = sigmoid(linear)
            active = linear * sig
            mix[spot, :] += mm((hidden * active).astype(bf16), picks)
            slope = sig + active * (1.0 - sig)
            linear_grad[spot, lanes] = (gate * hidden * slope).astype(bf16)
            weighed[spot, :] = (gate * active).astype(bf16)
        dwiden[:, lanes] = mm(xt[...], linear_grad[:, lanes])
        dnarrow[lanes, :] = mm(weighed[...], os[...], 0, 0)
        return 0

    lax.fori_loop(0, total // size, tile, 0)
    for at, out in ((0, out_own), (half, out_other)):
        out[:, :width] = mm(linear_grad[at : at + half, :], widen[...], 1, 1).astype(bf16)
        out[:, width:] = mix[at : at + half, :].astype(bf16)


def scatter_kernel(n, gate_count, *refs):
    pieces = refs[:n]
    dx, mix, from_own, from_other, home, away, gate_part = refs[n:]
    m, packed, width = pieces[0].shape
    rows = packed - AUX // 2
    capacity = from_own.shape[0] // (n * m)
    places = own_place(pieces, gate_count)
    live = lax.broadcasted_iota(jnp.int32, (rows, AUX), 1) < gate_count
    total = jnp.zeros(gate_part.shape, f32)
    for k in range(n):
        for b in range(m):
            piece = k * m + b
            out, to = (home, piece) if piece < home.shape[0] else (away, piece - home.shape[0])
            spot = slice(piece * capacity, (piece + 1) * capacity)
            full = slice(piece * rows, (piece + 1) * rows)
            side = side_of(pieces[k][b, rows:, :])
            value, dots = dx[full, :].astype(f32), mix[full, :].astype(f32)
            for (owner, first), source in zip(places, (from_own, from_other)):
                extra = mm(selector(side, gate_count, owner, capacity), source[spot, :], 0, 0)
                value += extra[:, :width]
                dots += mm(extra[:, width:].astype(bf16), gate_picks(first), 1, 1)
            out[to, :rows, :] = value.astype(bf16)
            turned = mm(eye(AUX), dots.astype(bf16), 1, 1).astype(bf16)
            out[to, rows:, :rows] = turned[: AUX // 2]
            out[to, rows:, rows:] = turned[AUX // 2 :]
            share = mm(side, eye(AUX), 0, 0)
            share = jnp.where(live, share, 0.0)
            share = share / jnp.sum(share, axis=1, keepdims=True)
            score = share * (dots - jnp.sum(share * dots, axis=1, keepdims=True))
            score = mm(eye(AUX), score.astype(bf16), 1, 1)[:gate_count]
            ids = side[gate_count : gate_count + 1, :].astype(f32)
            wide = score[:, None, :] * by_scenario(ids.astype(jnp.int32), total.shape[0] // gate_count)
            wide = wide.reshape(total.shape[0], rows).astype(bf16)
            total = total + mm(wide, pieces[k][b, :rows, :])
    gate_part[...] = total


def final_kernel(count, gate_count, *refs):
    parts = refs[:count]
    feats, sid, probs, gate, out = refs[count:]
    rows = feats.shape[0]
    total = parts[0][...].astype(f32)
    for part in parts[1:]:
        total = total + part[...].astype(f32)
    tail = total[rows:]
    half = tail.shape[1] // 2
    dots = jnp.concatenate([tail[:, :half], tail[:, half:]], axis=0)
    share = probs[...]
    live = lax.broadcasted_iota(jnp.int32, (AUX, rows), 0) < gate_count
    dots = jnp.where(live, dots, 0.0)
    score = share * (dots - jnp.sum(share * dots, axis=0, keepdims=True))
    score = score.astype(bf16).astype(f32)[:gate_count]
    wide = score[:, None, :] * by_scenario(sid[...], gate.shape[0] // gate_count)
    wide = wide.reshape(gate.shape[0], rows).astype(bf16)
    out[...] = (total[:rows] + mm(wide, gate[...], 0, 0)).astype(bf16)


def expand_grad_kernel(pieces, out):
    count, _, hidden = out.shape
    chips = pieces.shape[0]
    lanes = hidden // chips
    for k in range(count):
        for chip in range(chips):
            out[k, :, chip * lanes : (chip + 1) * lanes] = pieces[
                chip, :, k * lanes : (k + 1) * lanes
            ].astype(f32)


def body(
    features,
    scenario_id,
    scenario_pads,
    device_slot,
    mentor,
    gate_weight,
    expand,
    reduce,
    scenario_widen,
    scenario_narrow,
    head,
):
    rows, width = features.shape
    devices = lax.axis_size(AXIS)
    chips = devices // 2
    near = 2 ** ((chips.bit_length() - 1) // 2)
    far = chips // near
    n, m = near, far
    shared, depth, hidden = expand.shape
    lanes = hidden // chips
    scenarios, _, gates = gate_weight.shape
    capacity = rows // 4
    slot_width = scenario_widen.shape[2]
    classes = head.shape[1]
    all_rows = chips * rows
    assert gates + 6 <= AUX and rows == 128
    slots = chips * capacity
    hidden_chip = shared * lanes
    groups = [[2 * r + c for r in range(chips)] for c in range(2)]

    def send(value, mask):
        return lax.ppermute(value, AXIS, [(i, i ^ mask) for i in range(devices)])

    def gather(value):
        column = [value] + [send(value, 2 * near * b) for b in range(1, far)]
        stacked = jnp.stack(column)
        return [stacked] + [send(stacked, 2 * a) for a in range(1, near)]

    def total_of(value):
        value = value + send(value, 1)
        mask = 2
        while mask < devices:
            half = value.astype(bf16)
            value = half.astype(f32) + send(half, mask).astype(f32)
            mask *= 2
        return value

    sid = scenario_id.reshape(1, rows)
    gate = jnp.transpose(gate_weight, (2, 0, 1)).reshape(gates * scenarios, width)
    widen, narrow = scenario_widen[0], scenario_narrow[0]
    tiled = lanes % 128 == 0 and depth % 16 == 0
    if not tiled:
        expand = expand.reshape(shared, depth, chips, lanes).transpose(2, 1, 0, 3)
        expand = expand.reshape(chips, depth, hidden_chip)

    pack_rows = rows + AUX // 2
    pack, probs = call(
        functools.partial(prep_kernel, shared, hidden, slot_width),
        [struct((pack_rows, width), bf16), struct((AUX, rows), f32)],
        [scenario_pads, device_slot, features, sid, gate],
        [SCALARS] * 2 + [None] * 3,
        [pltpu.VMEM((AUX, rows), f32)],
        limit=FIRST,
    )
    column = [pack] + [send(pack, 2 * near * b) for b in range(1, far)]
    stacked = jnp.stack(column)
    stacked, expand = lax.optimization_barrier((stacked, expand))
    got = [stacked] + [send(stacked, 2 * a) for a in range(1, near)]
    (pieces,) = call(
        functools.partial(tile_kernel, tiled),
        [struct((chips, depth, hidden_chip), bf16)],
        [expand],
        limit=8,
    )
    w2a = reduce
    w2b = send(reduce, 1)
    w1a = lax.all_to_all(
        pieces, AXIS, split_axis=0, concat_axis=0, tiled=True, axis_index_groups=groups
    ).reshape(width // 2, hidden_chip)
    x_own, x_send = call(
        functools.partial(compact_kernel, n, gates, capacity),
        [struct((slots, width + 128), bf16)] * 2,
        got,
        limit=SMALL,
    )
    x_other = send(x_send, 1)
    out_own, out_send = call(
        functools.partial(scenario_forward_kernel, hidden),
        [struct((slots, width), bf16)] * 2,
        [x_own, x_other, widen, narrow],
        scratch=[pltpu.VMEM((2 * slots, slot_width), bf16)],
        limit=SMALL,
    )
    w1a, out_send = lax.optimization_barrier((w1a, out_send))
    out_other = send(out_send, 1)
    w1b = send(w1a, 1)
    weights = [w1a, w1b, w2a, w2b]
    weight_scratch = [
        pltpu.VMEM((width, hidden_chip), bf16),
        pltpu.VMEM((hidden_chip, width), bf16),
    ]

    def forward(pieces, start):
        count = len(pieces) * far
        (out,) = call(
            functools.partial(shared_forward_kernel, len(pieces), start, lanes, gates, depth),
            [struct((count, rows, width), bf16)],
            [got[0], *pieces, *weights, out_own, out_other],
            scratch=[
                pltpu.VMEM((count * rows, width), bf16),
                pltpu.VMEM((count * rows, AUX), bf16),
                *weight_scratch,
                pltpu.VMEM((count * rows, hidden_chip), bf16),
            ],
            limit=BIG,
        )
        return out

    away = forward(got[1:], far)
    home = forward(got[:1], 0)
    total = home.astype(f32)
    for a in range(1, near):
        total = total + send(away[(a - 1) * far : a * far], 2 * a).astype(f32)
    total = total.astype(bf16)
    layer_parts = [total[0]] + [send(total[b], 2 * near * b) for b in range(1, far)]
    logit_grad, head_part = call(
        functools.partial(head_kernel, len(layer_parts)),
        [struct((rows, classes), bf16), struct((width, classes), f32)],
        [*layer_parts, head, mentor],
        limit=8,
    )
    logits = gather(logit_grad)
    head_total = total_of(head_part)

    x_own, x_send = call(
        functools.partial(compact_kernel, n, gates, capacity),
        [struct((slots, width + 128 + classes), bf16)] * 2,
        [*got, *logits],
        limit=SMALL,
    )
    x_other = send(x_send, 1)
    dx, mix, dw1_keep, dw1_send, dw2_keep, dw2_send = call(
        functools.partial(shared_backward_kernel, n, lanes, depth),
        [
            struct((all_rows, width), bf16),
            struct((all_rows, AUX), f32),
            struct((width // 2, hidden_chip), bf16),
            struct((width // 2, hidden_chip), bf16),
            struct((shared, lanes // 2, width), f32),
            struct((shared, lanes // 2, width), bf16),
        ],
        [*got, *logits, head, *weights],
        scratch=[
            pltpu.VMEM((all_rows, width), bf16),
            pltpu.VMEM((width, all_rows), bf16),
            pltpu.VMEM((all_rows, AUX), bf16),
            *weight_scratch,
            pltpu.VMEM((all_rows, width), bf16),
            pltpu.VMEM((all_rows, hidden_chip), bf16),
            pltpu.VMEM((all_rows, min(TILE, hidden_chip)), bf16),
        ],
        limit=BIG,
    )
    dw1 = (dw1_keep.astype(f32) + send(dw1_send, 1).astype(f32)).astype(bf16)
    dw1, x_own = lax.optimization_barrier((dw1, x_own))
    dw1 = lax.all_to_all(
        dw1.reshape(chips, depth, hidden_chip),
        AXIS, split_axis=0, concat_axis=0, tiled=True, axis_index_groups=groups,
    )
    dx_own, dx_send, widen_grad, narrow_grad = call(
        functools.partial(scenario_backward_kernel, hidden),
        [struct((slots, width + 128), bf16)] * 2
        + [struct((width, slot_width), f32), struct((slot_width, width), f32)],
        [x_own, x_other, head, widen, narrow],
        None,
        [
            pltpu.VMEM((2 * slots, width + 128 + classes), bf16),
            pltpu.VMEM((width, 2 * slots), bf16),
            pltpu.VMEM((2 * slots, width), bf16),
            pltpu.VMEM((2 * slots, slot_width), bf16),
            pltpu.VMEM((2 * slots, min(TILE, slot_width)), bf16),
            pltpu.VMEM((2 * slots, 128), f32),
        ],
        limit=BIG,
    )
    dx_other = send(dx_send, 1)
    reduce_grad = dw2_keep + send(dw2_send, 1).astype(f32)
    dw1, dx_own = lax.optimization_barrier((dw1, dx_own))
    grad_home, grad_away, gate_part = call(
        functools.partial(scatter_kernel, n, gates),
        [
            struct((far, pack_rows, width), bf16),
            struct((chips - far, pack_rows, width), bf16),
            struct((gates * scenarios, width), f32),
        ],
        [*got, dx, mix, dx_own, dx_other],
        limit=SMALL,
    )
    total = grad_home.astype(f32)
    for a in range(1, near):
        total = total + send(grad_away[(a - 1) * far : a * far], 2 * a).astype(f32)
    total = total.astype(bf16)
    grad_parts = [total[0]] + [send(total[b], 2 * near * b) for b in range(1, far)]
    gate_total = total_of(gate_part).reshape(gates, scenarios, width)
    gate_total = jnp.transpose(gate_total, (1, 2, 0))
    if tiled:
        (expand_grad,) = call(
            expand_grad_kernel, [struct((shared, depth, hidden), f32)], [dw1], limit=8
        )
    else:
        expand_grad = dw1.reshape(chips, depth, shared, lanes).transpose(2, 1, 0, 3)
        expand_grad = expand_grad.reshape(shared, depth, hidden).astype(f32)

    (feature_grad,) = call(
        functools.partial(final_kernel, len(grad_parts), gates),
        [struct((rows, width), bf16)],
        [*grad_parts, features, sid, probs, gate],
        limit=8,
    )
    return (
        feature_grad,
        expand_grad,
        reduce_grad,
        widen_grad[None],
        narrow_grad[None],
        gate_total,
        head_total,
    )


def solution(mesh):
    placed = (
        P(("groups", "expert"), None),
        P(("groups", "expert")),
        P("groups"),
        P(),
        P(("groups", "expert"), None),
        P(),
        P(None, "expert", None),
        P(None, "expert", None),
        P("expert", None, None),
        P("expert", None, None),
        P(),
    )
    return jax.shard_map(
        body,
        mesh=mesh,
        in_specs=placed,
        out_specs=(
            P(("groups", "expert"), None),
            P("groups", "expert", None),
            P("groups", "expert", None),
            P(("groups", "expert"), None, None),
            P(("groups", "expert"), None, None),
            P("groups", None, None),
            P("groups", None),
        ),
        check_vma=False,
    )
```

```python
import functools

import jax
import jax.numpy as jnp
from jax import lax
from jax.experimental import pallas as pl
from jax.experimental.pallas import tpu as pltpu
from jax.sharding import PartitionSpec as P

AXIS = "expert"
TILE = 512
AUX = 32
bf16 = jnp.bfloat16
f32 = jnp.float32
CHUNK = 256
FIRST, SMALL, BIG = 60, 16, 32
COST = 100000


def mm(left, right, left_dim=1, right_dim=0):
    return lax.dot_general(
        left, right, (((left_dim,), (right_dim,)), ((), ())), preferred_element_type=f32
    )


def call(kernel, out_shapes, operands, in_specs=None, scratch=(), limit=48):
    specs = in_specs or [None] * len(operands)
    specs = [pl.BlockSpec(memory_space=pltpu.VMEM) if s is None else s for s in specs]
    return pl.pallas_call(
        kernel,
        out_shape=out_shapes,
        in_specs=specs,
        out_specs=[pl.BlockSpec(memory_space=pltpu.VMEM) for _ in out_shapes],
        scratch_shapes=list(scratch),
        compiler_params=pltpu.CompilerParams(vmem_limit_bytes=limit * 1024 * 1024),
        cost_estimate=pl.CostEstimate(flops=COST, bytes_accessed=COST, transcendentals=0),
    )(*operands)


SCALARS = pl.BlockSpec(memory_space=pltpu.SMEM)


def own_core():
    return lax.rem(lax.axis_index(AXIS), 2)


def struct(shape, kind):
    return jax.ShapeDtypeStruct(shape, kind)


def sigmoid(v):
    return 0.5 * (1.0 + jnp.tanh(0.5 * v))


def eye(size):
    rows = lax.broadcasted_iota(jnp.int32, (size, size), 0)
    cols = lax.broadcasted_iota(jnp.int32, (size, size), 1)
    return (rows == cols).astype(f32).astype(bf16)


def spread(tile, size, expert_lanes):
    rows = lax.broadcasted_iota(jnp.int32, (AUX, size), 0)
    lanes = lax.broadcasted_iota(jnp.int32, (AUX, size), 1) + tile * size
    first = rows * expert_lanes
    return ((lanes >= first) & (lanes < first + expert_lanes)).astype(f32).astype(bf16)


def turn_matrix(size, depth, core):
    place = lax.broadcasted_iota(jnp.int32, (size, size), 0)
    column = lax.broadcasted_iota(jnp.int32, (size, size), 1)
    half = size // 2
    other = place // half
    place = place - other * half
    chip = place // depth
    which = jnp.where(core == 0, other, 1 - other)
    return (column == (chip * 2 + which) * depth + (place - chip * depth)).astype(f32).astype(bf16)


def side_of(piece):
    half = piece.shape[1] // 2
    return jnp.concatenate([piece[:, :half], piece[:, half:]], axis=0)


def selector(side, gate_count, owner, capacity):
    wide = side.astype(f32)
    which = wide[gate_count : gate_count + 1, :]
    slot = wide[gate_count + 1 : gate_count + 2, :]
    ranks = lax.broadcasted_iota(jnp.int32, (capacity, side.shape[1]), 0).astype(f32)
    hit = (ranks == slot) & (which == owner)
    return hit.astype(f32).astype(bf16)


def placement(own_side, gate_count):
    wide = own_side.astype(f32)
    rows = [wide[gate_count + 2 + i : gate_count + 3 + i, :] for i in range(4)]
    return (rows[0], rows[1]), (rows[2], rows[3])


def gate_picks(first):
    shape = (AUX, first.shape[1])
    rows = lax.broadcasted_iota(jnp.int32, shape, 0)
    lanes = lax.broadcasted_iota(jnp.int32, shape, 1)
    return ((rows - lanes).astype(f32) == first).astype(f32).astype(bf16)


def by_scenario(ids, scenarios):
    labels = lax.broadcasted_iota(jnp.int32, (scenarios, ids.shape[1]), 0)
    return (labels == ids).astype(f32)[None]


def prep_kernel(shared, hidden, slot_width, pads, slots, feats, sid, gate, pack, probs, scr):
    scenarios = pads.shape[0]
    gate_count = gate.shape[0] // scenarios
    rows = feats.shape[0]
    x = feats[...]
    ids = sid[...]
    scr[...] = jnp.zeros_like(scr)
    pad = jnp.zeros((1, rows), f32)
    for s in range(scenarios):
        pad = pad + jnp.where(ids == s, pads[s].astype(f32), 0.0)
    logits = mm(gate[...], x, 1, 1).reshape(gate_count, scenarios, rows)
    own = jnp.sum(logits * by_scenario(ids, scenarios), axis=1)
    top = jnp.max(own, axis=0, keepdims=True)
    raised = jnp.exp(own - top)
    scr[:gate_count, :] = raised / jnp.sum(raised, axis=0, keepdims=True)
    probs[...] = scr[...]
    labels = lax.broadcasted_iota(jnp.int32, (AUX, rows), 0)
    member = (ids == labels).astype(f32)
    earlier = (
        lax.broadcasted_iota(jnp.int32, (rows, rows), 0)
        < lax.broadcasted_iota(jnp.int32, (rows, rows), 1)
    ).astype(f32).astype(bf16)
    rank = jnp.sum(mm(member.astype(bf16), earlier) * member, axis=0, keepdims=True)
    slot = jnp.where(rank < pad, rank, -1.0)
    scr[gate_count : gate_count + 1, :] = ids.astype(f32)
    scr[gate_count + 1 : gate_count + 2, :] = slot
    index = lax.axis_index(AXIS)
    group = slots.shape[0] // scenarios
    for i, device in enumerate((index, index + 1 - 2 * lax.rem(index, 2))):
        owned = slots[device]
        first = shared + lax.rem(owned, group) * slot_width // hidden
        for j, value in enumerate((owned // group, first)):
            at = gate_count + 2 + 2 * i + j
            scr[at : at + 1, :] = jnp.zeros((1, rows), f32) + value.astype(f32)
    side = scr[...].astype(bf16)
    pack[:rows, :] = x
    pack[rows:, :rows] = side[: AUX // 2]
    pack[rows:, rows:] = side[AUX // 2 :]


def tile_kernel(tiled, expand, pieces):
    if tiled:
        chips, _, total = pieces.shape
        count = expand.shape[0]
        lanes = total // count
        for k in range(count):
            for chip in range(chips):
                pieces[chip, :, k * lanes : (k + 1) * lanes] = expand[
                    k, :, chip * lanes : (chip + 1) * lanes
                ]
    else:
        pieces[...] = expand[...]


def own_place(pieces, gate_count):
    return placement(side_of(pieces[0][0, pieces[0].shape[1] - AUX // 2 :, :]), gate_count)


def compact_kernel(n, gate_count, capacity, *refs):
    pieces, logits, outs = refs[:n], refs[n:-2], refs[-2:]
    m = pieces[0].shape[0]
    rows = pieces[0].shape[1] - AUX // 2
    width = pieces[0].shape[2]
    places = own_place(pieces, gate_count)
    for k in range(n):
        for b in range(m):
            x = pieces[k][b, :rows, :]
            side = side_of(pieces[k][b, rows:, :])
            spot = slice((k * m + b) * capacity, (k * m + b + 1) * capacity)
            for (owner, first), out in zip(places, outs):
                sel = selector(side, gate_count, owner, capacity)
                out[spot, :width] = mm(sel, x).astype(bf16)
                gates = mm(sel, side, 1, 1).astype(bf16)
                out[spot, width : width + rows] = mm(gates, gate_picks(first)).astype(bf16)
                if logits:
                    out[spot, width + rows :] = mm(sel, logits[k][b]).astype(bf16)


def chosen_gate(x, width, expert):
    gates = x[:, width : width + 128].astype(f32)
    lanes = lax.broadcasted_iota(jnp.int32, gates.shape, 1)
    return jnp.sum(jnp.where(lanes == expert, gates, 0.0), axis=1, keepdims=True)


def hidden_lanes(j, size):
    return pl.ds(pl.multiple_of(j * size, size), size)


def scenario_forward_kernel(hidden, own, other, widen, narrow, out_own, out_other, gated):
    half, width = out_own.shape
    total = widen.shape[1]
    size, chunk = min(TILE, total), min(half, max(CHUNK, half // 2))

    def tile(j, _):
        lanes = hidden_lanes(j, size)
        for base, source in ((0, own), (half, other)):
            for at in range(0, half, chunk):
                x = source[at : at + chunk, :]
                gate = chosen_gate(x, width, (j * size) // hidden)
                linear = mm(x[:, :width], widen[:, lanes])
                spot = slice(base + at, base + at + chunk)
                gated[spot, lanes] = (gate * (linear * sigmoid(linear))).astype(bf16)
        return 0

    lax.fori_loop(0, total // size, tile, 0, unroll=True)
    out_own[...] = mm(gated[:half, :], narrow[...]).astype(bf16)
    out_other[...] = mm(gated[half:, :], narrow[...]).astype(bf16)


def put(outs, split, k, b, value, rows=slice(None), lanes=slice(None)):
    out, at, count = (outs[0], b, split) if b < split else (outs[1], b - split, None)
    count = count or outs[1].shape[0] // (outs[0].shape[0] // split)
    out[k * count + at, rows, lanes] = value


def unpack(pieces, turn, xs, gates, xt=None):
    m, packed, _ = pieces[0].shape
    rows = packed - AUX // 2
    for k in range(len(pieces)):
        for b in range(m):
            spot = slice((k * m + b) * rows, (k * m + b + 1) * rows)
            x = pieces[k][b, :rows, :]
            xs[spot, :] = mm(x, turn, 1, 1).astype(bf16)
            gates[spot, :] = mm(side_of(pieces[k][b, rows:, :]), eye(AUX), 0, 0).astype(bf16)
            if xt is not None:
                xt[:, spot] = mm(turn, x, 1, 1).astype(bf16)


def join_weights(w1a, w1b, w2a, w2b, w1, w2):
    half = w1a.shape[0]
    w1[:half, :] = w1a[...]
    w1[half:, :] = w1b[...]
    experts, part, _ = w2a.shape
    core = own_core()
    for k in range(experts):
        mine, theirs = w2a[k], w2b[k]
        w2[2 * k * part : (2 * k + 1) * part, :] = jnp.where(core == 0, mine, theirs)
        w2[(2 * k + 1) * part : 2 * (k + 1) * part, :] = jnp.where(core == 0, theirs, mine)


def shared_forward_kernel(n, start, split, gate_rows, gate_count, depth, *refs):
    own, pieces = refs[0], refs[1 : n + 1]
    w1a, w1b, w2a, w2b, from_own, from_other, *outs, xs, gates, w1, w2, gated = refs[n + 1 :]
    join_weights(w1a, w1b, w2a, w2b, w1, w2)
    unpack(pieces, turn_matrix(w1.shape[0], depth, own_core()), xs, gates)
    m, packed, _ = pieces[0].shape
    count, rows = n * m, packed - AUX // 2
    capacity = from_own.shape[0] // (w1.shape[0] // (2 * depth))
    places = own_place([own], gate_count)
    total = count * rows
    size, chunk = min(TILE, w1.shape[1]), min(total, max(CHUNK, total // 4))

    def tile(j, _):
        lanes = hidden_lanes(j, size)
        picks = spread(j, size, gate_rows)
        for at in range(0, total, chunk):
            spot = slice(at, at + chunk)
            linear = mm(xs[spot, :], w1[:, lanes])
            active = linear * sigmoid(linear)
            gated[spot, lanes] = (mm(gates[spot, :], picks) * active).astype(bf16)
        return 0

    lax.fori_loop(0, w1.shape[1] // size, tile, 0, unroll=True)
    for at in range(0, total, chunk):
        mixed = mm(gated[at : at + chunk, :], w2[...])
        for piece in range(at // rows, (at + chunk) // rows):
            side = side_of(pieces[piece // m][piece % m, rows:, :])
            spot = slice((start + piece) * capacity, (start + piece + 1) * capacity)
            value = mixed[piece * rows - at : (piece + 1) * rows - at]
            for (owner, _), source in zip(places, (from_own, from_other)):
                value += mm(selector(side, gate_count, owner, capacity), source[spot, :], 0, 0)
            put(outs, split, piece // m, piece % m, value.astype(bf16))


def softmax(v):
    raised = jnp.exp(v - jnp.max(v, axis=1, keepdims=True))
    return raised / jnp.sum(raised, axis=1, keepdims=True)


def head_kernel(count, *refs):
    parts = refs[:count]
    head, mentor, grad, head_part = refs[count:]
    layer = parts[0][...].astype(f32)
    for part in parts[1:]:
        layer = layer + part[...].astype(f32)
    rounded = layer.astype(bf16)
    student = mm(rounded, head[...])
    value = (2.0 * (softmax(student * 0.5) - softmax(mentor[...] * 0.5))).astype(bf16)
    grad[...] = value
    head_part[...] = mm(rounded, value, 0, 0)


def shared_backward_kernel(n, gate_rows, depth, *refs):
    pieces, logits = refs[:n], refs[n : 2 * n]
    head, w1a, w1b, w2a, w2b = refs[2 * n : 2 * n + 5]
    dx, mix, keep, sent, keep2, sent2 = refs[2 * n + 5 : 2 * n + 11]
    xp, xpt, gates, w1, w2, os, linear_grad, weighed = refs[2 * n + 11 :]
    core = own_core()
    turn = turn_matrix(w1.shape[0], depth, core)
    join_weights(w1a, w1b, w2a, w2b, w1, w2)
    unpack(pieces, turn, xp, gates, xpt)
    m, rows, _ = logits[0].shape
    for k in range(n):
        for b in range(m):
            at = (k * m + b) * rows
            os[at : at + rows, :] = mm(logits[k][b], head[...], 1, 1).astype(bf16)
    total = n * m * rows
    size, chunk = weighed.shape[1], min(total, max(CHUNK, total // 4))
    half, part = keep.shape[0], keep2.shape[1]
    mix[...] = jnp.zeros_like(mix)

    def tile(j, _):
        lanes = hidden_lanes(j, size)
        picks = spread(j, size, gate_rows)
        for at in range(0, total, chunk):
            spot = slice(at, at + chunk)
            linear = mm(xp[spot, :], w1[:, lanes])
            hidden = mm(os[spot, :], w2[lanes, :], 1, 1)
            gate = mm(gates[spot, :], picks)
            sig = sigmoid(linear)
            active = linear * sig
            product = hidden * active
            if gate_rows % 128 == 0:
                column = lax.broadcasted_iota(jnp.int32, (chunk, AUX), 1) - j * (size // gate_rows)
                dots = jnp.zeros((chunk, AUX), f32)
                for e in range(size // gate_rows):
                    part_of = product[:, e * gate_rows : (e + 1) * gate_rows]
                    dots = jnp.where(column == e, jnp.sum(part_of, axis=1, keepdims=True), dots)
            else:
                dots = mm(product.astype(bf16), picks, 1, 1)
            mix[spot, :] += dots
            slope = sig + active * (1.0 - sig)
            linear_grad[spot, lanes] = (gate * hidden * slope).astype(bf16)
            weighed[spot, :] = (gate * active).astype(bf16)
        first = mm(xpt[...], linear_grad[:, lanes])
        keep[:, lanes] = first[:half].astype(keep.dtype)
        sent[:, lanes] = first[half:].astype(bf16)
        second = mm(weighed[...], os[...], 0, 0)
        for e in range(size // gate_rows):
            low = second[e * gate_rows : e * gate_rows + part]
            high = second[e * gate_rows + part : (e + 1) * gate_rows]
            k = j * (size // gate_rows) + e
            keep2[k] = jnp.where(core == 0, low, high)
            sent2[k] = jnp.where(core == 0, high, low).astype(bf16)
        return 0

    lax.fori_loop(0, w1.shape[1] // size, tile, 0, unroll=True)
    chunk = min(total, 1024)
    for at in range(0, total, chunk):
        spot = slice(at, at + chunk)
        value = mm(linear_grad[spot, :], w1[...], 1, 1).astype(bf16)
        dx[spot, :] = mm(value, turn).astype(bf16)


def scenario_backward_kernel(
    hidden_units, own, other, head, widen, narrow,
    out_own, out_other, dwiden, dnarrow, xs, xt, os, linear_grad, weighed, mix,
):
    half = out_own.shape[0]
    width = narrow.shape[1]
    total = widen.shape[1]
    xs[:half, :] = own[...]
    xs[half:, :] = other[...]
    os[...] = mm(xs[:, width + 128 :], head[...], 1, 1).astype(bf16)
    mix[...] = jnp.zeros_like(mix)
    size, chunk = min(TILE, total), min(2 * half, max(CHUNK, half // 2))
    for at in range(0, 2 * half, chunk):
        xt[:, at : at + chunk] = mm(eye(width), xs[at : at + chunk, :width], 1, 1).astype(bf16)

    def tile(j, _):
        lanes = hidden_lanes(j, size)
        column = (j * size) // hidden_units
        lane = lax.broadcasted_iota(jnp.int32, (chunk, mix.shape[1]), 1)
        for at in range(0, 2 * half, chunk):
            spot = slice(at, at + chunk)
            x = xs[spot, :]
            gate = chosen_gate(x, width, column)
            linear = mm(x[:, :width], widen[:, lanes])
            hidden = mm(os[spot, :], narrow[lanes, :], 1, 1)
            sig = sigmoid(linear)
            active = linear * sig
            product = jnp.sum(hidden * active, axis=1, keepdims=True)
            mix[spot, :] += jnp.where(lane == column, product, 0.0)
            slope = sig + active * (1.0 - sig)
            linear_grad[spot, lanes] = (gate * hidden * slope).astype(bf16)
            weighed[spot, :] = (gate * active).astype(bf16)
        dwiden[:, lanes] = mm(xt[...], linear_grad[:, lanes])
        dnarrow[lanes, :] = mm(weighed[...], os[...], 0, 0)
        return 0

    lax.fori_loop(0, total // size, tile, 0, unroll=True)
    for at, out in ((0, out_own), (half, out_other)):
        out[:, :width] = mm(linear_grad[at : at + half, :], widen[...], 1, 1).astype(bf16)
        out[:, width:] = mix[at : at + half, :].astype(bf16)


def scatter_kernel(n, split, gate_count, *refs):
    pieces = refs[:n]
    dx, mix, from_own, from_other, home, *away, mix_out = refs[n:]
    m, packed, width = pieces[0].shape
    rows = packed - AUX // 2
    capacity = from_own.shape[0] // (n * m)
    places = own_place(pieces, gate_count)
    picks = [gate_picks(first) for _, first in places]
    for k in range(n):
        for b in range(m):
            piece = k * m + b
            spot = slice(piece * capacity, (piece + 1) * capacity)
            full = slice(piece * rows, (piece + 1) * rows)
            side = side_of(pieces[k][b, rows:, :])
            value = dx[full, :].astype(f32)
            dots = mm(eye(AUX), mix[full, :].astype(bf16), 1, 1)
            for (owner, _), pick, source in zip(places, picks, (from_own, from_other)):
                sel = selector(side, gate_count, owner, capacity)
                extra = mm(sel, source[spot, :], 0, 0)
                value += extra[:, :width]
                dots += mm(pick, extra[:, width:].astype(bf16), 1, 1)
            turned = dots.astype(bf16)
            mix_out[piece] = turned
            outs, at, line = (away, k - 1, split) if k else ([home], 0, m)
            put(outs, line, at, b, value.astype(bf16), slice(rows))
            put(outs, line, at, b, turned[: AUX // 2], slice(rows, None), slice(rows))
            put(outs, line, at, b, turned[AUX // 2 :], slice(rows, None), slice(rows, None))


def gate_kernel(n, gate_count, *refs):
    pieces, mix, out = refs[:n], refs[n], refs[n + 1]
    m, packed, _ = pieces[0].shape
    rows = packed - AUX // 2
    live = lax.broadcasted_iota(jnp.int32, (AUX, rows), 0) < gate_count
    count = out.shape[0] // 2
    total = jnp.zeros((count, 2 * out.shape[1]), f32)
    for k in range(n):
        for b in range(m):
            side = side_of(pieces[k][b, rows:, :]).astype(f32)
            dots = mix[k * m + b].astype(f32)
            share = jnp.where(live, side, 0.0)
            share = share / jnp.sum(share, axis=0, keepdims=True)
            score = share * (dots - jnp.sum(share * dots, axis=0, keepdims=True))
            ids = side[gate_count : gate_count + 1, :].astype(jnp.int32)
            wide = score[:gate_count, None, :] * by_scenario(ids, count // gate_count)
            wide = wide.reshape(count, rows).astype(bf16)
            total = total + mm(wide, pieces[k][b, :rows, :])
    out[:count, :] = total[:, : out.shape[1]]
    out[count:, :] = total[:, out.shape[1] :]


def final_kernel(count, gate_count, *refs):
    parts = refs[:count]
    feats, sid, probs, gate, out = refs[count:]
    rows = feats.shape[0]
    total = parts[0][...].astype(f32)
    for part in parts[1:]:
        total = total + part[...].astype(f32)
    tail = total[rows:]
    half = tail.shape[1] // 2
    dots = jnp.concatenate([tail[:, :half], tail[:, half:]], axis=0)
    share = probs[...]
    live = lax.broadcasted_iota(jnp.int32, (AUX, rows), 0) < gate_count
    dots = jnp.where(live, dots, 0.0)
    score = share * (dots - jnp.sum(share * dots, axis=0, keepdims=True))
    score = score.astype(bf16).astype(f32)[:gate_count]
    wide = score[:, None, :] * by_scenario(sid[...], gate.shape[0] // gate_count)
    wide = wide.reshape(gate.shape[0], rows).astype(bf16)
    out[...] = (total[:rows] + mm(wide, gate[...], 0, 0)).astype(bf16)


def expand_grad_kernel(pieces, out):
    count, _, hidden = out.shape
    chips = pieces.shape[0]
    lanes = hidden // chips
    for k in range(count):
        for chip in range(chips):
            out[k, :, chip * lanes : (chip + 1) * lanes] = pieces[
                chip, :, k * lanes : (k + 1) * lanes
            ].astype(f32)


def body(
    features,
    scenario_id,
    scenario_pads,
    device_slot,
    mentor,
    gate_weight,
    expand,
    reduce,
    scenario_widen,
    scenario_narrow,
    head,
):
    rows, width = features.shape
    devices = lax.axis_size(AXIS)
    chips = devices // 2
    near = 2 ** ((chips.bit_length() - 1) // 2)
    far = chips // near
    n, m = near, far
    shared, depth, hidden = expand.shape
    lanes = hidden // chips
    scenarios, _, gates = gate_weight.shape
    capacity = rows // 4
    slot_width = scenario_widen.shape[2]
    classes = head.shape[1]
    all_rows = chips * rows
    assert gates + 6 <= AUX and rows == 128
    slots = chips * capacity
    hidden_chip = shared * lanes
    groups = [[2 * r + c for r in range(chips)] for c in range(2)]

    def send(value, mask):
        return lax.ppermute(value, AXIS, [(i, i ^ mask) for i in range(devices)])

    def gather(value):
        column = [value] + [send(value, 2 * near * b) for b in range(1, far)]
        stacked = jnp.stack(column)
        return [stacked] + [send(stacked, 2 * a) for a in range(1, near)]

    def total_of(value, mask, end):
        if mask == 1:
            value = value + send(value, 1)
            mask = 2
        while mask < end:
            half = value.astype(bf16)
            value = half.astype(f32) + send(half, mask).astype(f32)
            mask *= 2
        return value

    sid = scenario_id.reshape(1, rows)
    gate = jnp.transpose(gate_weight, (2, 0, 1)).reshape(gates * scenarios, width)
    widen, narrow = scenario_widen[0], scenario_narrow[0]
    tiled = lanes % 128 == 0 and depth % 16 == 0
    if not tiled:
        expand = expand.reshape(shared, depth, chips, lanes).transpose(2, 1, 0, 3)
        expand = expand.reshape(chips, depth, hidden_chip)

    pack_rows = rows + AUX // 2
    pack, probs = call(
        functools.partial(prep_kernel, shared, hidden, slot_width),
        [struct((pack_rows, width), bf16), struct((AUX, rows), f32)],
        [scenario_pads, device_slot, features, sid, gate],
        [SCALARS] * 2 + [None] * 3,
        [pltpu.VMEM((AUX, rows), f32)],
        limit=FIRST,
    )
    (pieces,) = call(
        functools.partial(tile_kernel, tiled),
        [struct((chips, depth, hidden_chip), bf16)],
        [expand],
        limit=SMALL,
    )
    column = [pack] + [send(pack, 2 * near * b) for b in range(1, far)]
    stacked = jnp.stack(column)
    stacked, pieces = lax.optimization_barrier((stacked, pieces))
    got = [stacked] + [send(stacked, 2 * a) for a in range(1, near)]
    w2a = reduce
    w2b = send(reduce, 1)
    w1a = lax.all_to_all(
        pieces, AXIS, split_axis=0, concat_axis=0, tiled=True, axis_index_groups=groups
    ).reshape(width // 2, hidden_chip)
    x_own, x_send = call(
        functools.partial(compact_kernel, n, gates, capacity),
        [struct((slots, width + 128), bf16)] * 2,
        got,
        limit=SMALL,
    )
    x_other = send(x_send, 1)
    out_own, out_send = call(
        functools.partial(scenario_forward_kernel, hidden),
        [struct((slots, width), bf16)] * 2,
        [x_own, x_other, widen, narrow],
        scratch=[pltpu.VMEM((2 * slots, slot_width), bf16)],
        limit=SMALL,
    )
    w1a, out_send = lax.optimization_barrier((w1a, out_send))
    out_other = send(out_send, 1)
    w1b = send(w1a, 1)
    weights = [w1a, w1b, w2a, w2b]
    weight_scratch = [
        pltpu.VMEM((width, hidden_chip), bf16),
        pltpu.VMEM((hidden_chip, width), bf16),
    ]

    def forward(pieces, start, lines):
        count = len(pieces) * far
        return call(
            functools.partial(
                shared_forward_kernel, len(pieces), start, lines[0], lanes, gates, depth
            ),
            [struct((len(pieces) * line, rows, width), bf16) for line in lines],
            [got[0], *pieces, *weights, out_own, out_other],
            scratch=[
                pltpu.VMEM((count * rows, width), bf16),
                pltpu.VMEM((count * rows, AUX), bf16),
                *weight_scratch,
                pltpu.VMEM((count * rows, hidden_chip), bf16),
            ],
            limit=BIG,
        )

    split = far // 2
    lines = (split, far - split)
    away = forward(got[1:], far, lines)
    (home,) = forward(got[:1], 0, (far,))

    def along_near(home, away):
        count = home.shape[0]
        total = home.astype(f32)
        for a in range(1, near):
            total = total + send(away[(a - 1) * count : a * count], 2 * a).astype(f32)
        return total.astype(bf16)

    def along_far(low, high):
        column = [low[b] for b in range(split)] + [high[b] for b in range(far - split)]
        return [column[0]] + [send(column[b], 2 * near * b) for b in range(1, far)]

    high = along_near(home[split:], away[1])
    low = along_near(home[:split], away[0])
    layer_parts = along_far(low, high)
    logit_grad, head_part = call(
        functools.partial(head_kernel, len(layer_parts)),
        [struct((rows, classes), bf16), struct((width, classes), f32)],
        [*layer_parts, head, mentor],
        limit=8,
    )
    logits = gather(logit_grad)
    head_part = total_of(head_part, 1, 2 * near)
    logits[0], head_part = lax.optimization_barrier((logits[0], head_part))

    x_own, x_send = call(
        functools.partial(compact_kernel, n, gates, capacity),
        [struct((slots, width + 128 + classes), bf16)] * 2,
        [*got, *logits],
        limit=SMALL,
    )
    logits[0], x_send = lax.optimization_barrier((logits[0], x_send))
    x_other = send(x_send, 1)
    dx, mix, dw1_keep, dw1_send, dw2_keep, dw2_send = call(
        functools.partial(shared_backward_kernel, n, lanes, depth),
        [
            struct((all_rows, width), bf16),
            struct((all_rows, AUX), f32),
            struct((width // 2, hidden_chip), bf16),
            struct((width // 2, hidden_chip), bf16),
            struct((shared, lanes // 2, width), f32),
            struct((shared, lanes // 2, width), bf16),
        ],
        [*got, *logits, head, *weights],
        scratch=[
            pltpu.VMEM((all_rows, width), bf16),
            pltpu.VMEM((width, all_rows), bf16),
            pltpu.VMEM((all_rows, AUX), bf16),
            *weight_scratch,
            pltpu.VMEM((all_rows, width), bf16),
            pltpu.VMEM((all_rows, hidden_chip), bf16),
            pltpu.VMEM((all_rows, min(256, hidden_chip)), bf16),
        ],
        limit=BIG,
    )
    dw1 = (dw1_keep.astype(f32) + send(dw1_send, 1).astype(f32)).astype(bf16)
    dw1, x_own = lax.optimization_barrier((dw1, x_own))
    dw1 = lax.all_to_all(
        dw1.reshape(chips, depth, hidden_chip),
        AXIS, split_axis=0, concat_axis=0, tiled=True, axis_index_groups=groups,
    )
    dx_own, dx_send, widen_grad, narrow_grad = call(
        functools.partial(scenario_backward_kernel, hidden),
        [struct((slots, width + 128), bf16)] * 2
        + [struct((width, slot_width), f32), struct((slot_width, width), f32)],
        [x_own, x_other, head, widen, narrow],
        None,
        [
            pltpu.VMEM((2 * slots, width + 128 + classes), bf16),
            pltpu.VMEM((width, 2 * slots), bf16),
            pltpu.VMEM((2 * slots, width), bf16),
            pltpu.VMEM((2 * slots, slot_width), bf16),
            pltpu.VMEM((2 * slots, min(TILE, slot_width)), bf16),
            pltpu.VMEM((2 * slots, 128), f32),
        ],
        limit=BIG,
    )
    dx_other = send(dx_send, 1)
    reduce_grad = dw2_keep + send(dw2_send, 1).astype(f32)
    grad_home, low, high, mix = call(
        functools.partial(scatter_kernel, n, split, gates),
        [
            struct((far, pack_rows, width), bf16),
            *[struct(((near - 1) * line, pack_rows, width), bf16) for line in lines],
            struct((chips, AUX, rows), bf16),
        ],
        [*got, dx, mix, dx_own, dx_other],
        limit=SMALL,
    )
    (gate_part,) = call(
        functools.partial(gate_kernel, n, gates),
        [struct((2 * gates * scenarios, width // 2), f32)],
        [*got, mix],
        limit=SMALL,
    )
    gate_part = total_of(gate_part, 1, 2 * near)
    low, high, gate_part, dw1 = lax.optimization_barrier((low, high, gate_part, dw1))
    high = along_near(grad_home[split:], high)
    low = along_near(grad_home[:split], low)
    grad_parts = along_far(low, high)
    count = gate_part.shape[0]
    if classes == width // 2:
        sums = total_of(jnp.concatenate([gate_part, head_part]), 2 * near, devices)
        gate_total, head_total = sums[:count], sums[count:]
    else:
        gate_total = total_of(gate_part, 2 * near, devices)
        head_total = total_of(head_part, 2 * near, devices)
    halves = [gate_total[: count // 2], gate_total[count // 2 :]]
    gate_total = jnp.concatenate(halves, axis=1).reshape(gates, scenarios, width)
    gate_total = jnp.transpose(gate_total, (1, 2, 0))
    if tiled:
        (expand_grad,) = call(
            expand_grad_kernel, [struct((shared, depth, hidden), f32)], [dw1], limit=8
        )
    else:
        expand_grad = dw1.reshape(chips, depth, shared, lanes).transpose(2, 1, 0, 3)
        expand_grad = expand_grad.reshape(shared, depth, hidden).astype(f32)

    (feature_grad,) = call(
        functools.partial(final_kernel, len(grad_parts), gates),
        [struct((rows, width), bf16)],
        [*grad_parts, features, sid, probs, gate],
        limit=8,
    )
    return (
        feature_grad,
        expand_grad,
        reduce_grad,
        widen_grad[None],
        narrow_grad[None],
        gate_total,
        head_total,
    )


def solution(mesh):
    placed = (
        P(("groups", "expert"), None),
        P(("groups", "expert")),
        P("groups"),
        P(),
        P(("groups", "expert"), None),
        P(),
        P(None, "expert", None),
        P(None, "expert", None),
        P("expert", None, None),
        P("expert", None, None),
        P(),
    )
    return jax.shard_map(
        body,
        mesh=mesh,
        in_specs=placed,
        out_specs=(
            P(("groups", "expert"), None),
            P("groups", "expert", None),
            P("groups", "expert", None),
            P(("groups", "expert"), None, None),
            P(("groups", "expert"), None, None),
            P("groups", None, None),
            P("groups", None),
        ),
        check_vma=False,
    )
```

```python
import functools

import jax
import jax.numpy as jnp
from jax import lax
from jax.experimental import pallas as pl
from jax.experimental.pallas import tpu as pltpu
from jax.sharding import PartitionSpec as P

AXIS = "expert"
TILE = 512
AUX = 32
bf16 = jnp.bfloat16
f32 = jnp.float32
CHUNK = 256
FIRST, SMALL, BIG = 60, 16, 32
COST = 100000


def mm(left, right, left_dim=1, right_dim=0):
    return lax.dot_general(
        left, right, (((left_dim,), (right_dim,)), ((), ())), preferred_element_type=f32
    )


def call(kernel, out_shapes, operands, in_specs=None, scratch=(), limit=48):
    specs = in_specs or [None] * len(operands)
    specs = [pl.BlockSpec(memory_space=pltpu.VMEM) if s is None else s for s in specs]
    return pl.pallas_call(
        kernel,
        out_shape=out_shapes,
        in_specs=specs,
        out_specs=[pl.BlockSpec(memory_space=pltpu.VMEM) for _ in out_shapes],
        scratch_shapes=list(scratch),
        compiler_params=pltpu.CompilerParams(vmem_limit_bytes=limit * 1024 * 1024),
        cost_estimate=pl.CostEstimate(flops=COST, bytes_accessed=COST, transcendentals=0),
    )(*operands)


SCALARS = pl.BlockSpec(memory_space=pltpu.SMEM)


def own_core():
    return lax.rem(lax.axis_index(AXIS), 2)


def struct(shape, kind):
    return jax.ShapeDtypeStruct(shape, kind)


def sigmoid(v):
    return 0.5 * (1.0 + jnp.tanh(0.5 * v))


def eye(size):
    rows = lax.broadcasted_iota(jnp.int32, (size, size), 0)
    cols = lax.broadcasted_iota(jnp.int32, (size, size), 1)
    return (rows == cols).astype(f32).astype(bf16)


def spread(tile, size, expert_lanes):
    rows = lax.broadcasted_iota(jnp.int32, (AUX, size), 0)
    lanes = lax.broadcasted_iota(jnp.int32, (AUX, size), 1) + tile * size
    first = rows * expert_lanes
    return ((lanes >= first) & (lanes < first + expert_lanes)).astype(f32).astype(bf16)


def turn_matrix(size, depth, core):
    place = lax.broadcasted_iota(jnp.int32, (size, size), 0)
    column = lax.broadcasted_iota(jnp.int32, (size, size), 1)
    half = size // 2
    other = place // half
    place = place - other * half
    chip = place // depth
    which = jnp.where(core == 0, other, 1 - other)
    return (column == (chip * 2 + which) * depth + (place - chip * depth)).astype(f32).astype(bf16)


def side_of(piece):
    half = piece.shape[1] // 2
    return jnp.concatenate([piece[:, :half], piece[:, half:]], axis=0)


def selector(side, gate_count, owner, capacity):
    wide = side.astype(f32)
    which = wide[gate_count : gate_count + 1, :]
    slot = wide[gate_count + 1 : gate_count + 2, :]
    ranks = lax.broadcasted_iota(jnp.int32, (capacity, side.shape[1]), 0).astype(f32)
    hit = (ranks == slot) & (which == owner)
    return hit.astype(f32).astype(bf16)


def placement(own_side, gate_count):
    wide = own_side.astype(f32)
    rows = [wide[gate_count + 2 + i : gate_count + 3 + i, :] for i in range(4)]
    return (rows[0], rows[1]), (rows[2], rows[3])


def gate_picks(first):
    shape = (AUX, first.shape[1])
    rows = lax.broadcasted_iota(jnp.int32, shape, 0)
    lanes = lax.broadcasted_iota(jnp.int32, shape, 1)
    return ((rows - lanes).astype(f32) == first).astype(f32).astype(bf16)


def by_scenario(ids, scenarios):
    labels = lax.broadcasted_iota(jnp.int32, (scenarios, ids.shape[1]), 0)
    return (labels == ids).astype(f32)[None]


def prep_kernel(shared, hidden, slot_width, pads, slots, feats, sid, gate, pack, probs, scr):
    scenarios = pads.shape[0]
    gate_count = gate.shape[0] // scenarios
    rows = feats.shape[0]
    x = feats[...]
    ids = sid[...]
    scr[...] = jnp.zeros_like(scr)
    pad = jnp.zeros((1, rows), f32)
    for s in range(scenarios):
        pad = pad + jnp.where(ids == s, pads[s].astype(f32), 0.0)
    logits = mm(gate[...], x, 1, 1).reshape(gate_count, scenarios, rows)
    own = jnp.sum(logits * by_scenario(ids, scenarios), axis=1)
    top = jnp.max(own, axis=0, keepdims=True)
    raised = jnp.exp(own - top)
    scr[:gate_count, :] = raised / jnp.sum(raised, axis=0, keepdims=True)
    probs[...] = scr[...]
    labels = lax.broadcasted_iota(jnp.int32, (AUX, rows), 0)
    member = (ids == labels).astype(f32)
    earlier = (
        lax.broadcasted_iota(jnp.int32, (rows, rows), 0)
        < lax.broadcasted_iota(jnp.int32, (rows, rows), 1)
    ).astype(f32).astype(bf16)
    rank = jnp.sum(mm(member.astype(bf16), earlier) * member, axis=0, keepdims=True)
    slot = jnp.where(rank < pad, rank, -1.0)
    scr[gate_count : gate_count + 1, :] = ids.astype(f32)
    scr[gate_count + 1 : gate_count + 2, :] = slot
    index = lax.axis_index(AXIS)
    group = slots.shape[0] // scenarios
    for i, device in enumerate((index, index + 1 - 2 * lax.rem(index, 2))):
        owned = slots[device]
        first = shared + lax.rem(owned, group) * slot_width // hidden
        for j, value in enumerate((owned // group, first)):
            at = gate_count + 2 + 2 * i + j
            scr[at : at + 1, :] = jnp.zeros((1, rows), f32) + value.astype(f32)
    side = scr[...].astype(bf16)
    pack[:rows, :] = x
    pack[rows:, :rows] = side[: AUX // 2]
    pack[rows:, rows:] = side[AUX // 2 :]


def tile_kernel(tiled, expand, pieces):
    if tiled:
        chips, _, total = pieces.shape
        count = expand.shape[0]
        lanes = total // count
        for k in range(count):
            for chip in range(chips):
                pieces[chip, :, k * lanes : (k + 1) * lanes] = expand[
                    k, :, chip * lanes : (chip + 1) * lanes
                ]
    else:
        pieces[...] = expand[...]


def own_place(pieces, gate_count):
    return placement(side_of(pieces[0][0, pieces[0].shape[1] - AUX // 2 :, :]), gate_count)


def compact_kernel(n, gate_count, capacity, *refs):
    own, pieces, logits, outs = refs[0], refs[1 : n + 1], refs[n + 1 : -2], refs[-2:]
    m = pieces[0].shape[0]
    rows = pieces[0].shape[1] - AUX // 2
    width = pieces[0].shape[2]
    places = own_place([own], gate_count)
    for k in range(n):
        for b in range(m):
            x = pieces[k][b, :rows, :]
            side = side_of(pieces[k][b, rows:, :])
            spot = slice((k * m + b) * capacity, (k * m + b + 1) * capacity)
            for (owner, first), out in zip(places, outs):
                sel = selector(side, gate_count, owner, capacity)
                out[spot, :width] = mm(sel, x).astype(bf16)
                gates = mm(sel, side, 1, 1).astype(bf16)
                out[spot, width : width + rows] = mm(gates, gate_picks(first)).astype(bf16)
                if logits:
                    out[spot, width + rows :] = mm(sel, logits[k][b]).astype(bf16)


def chosen_gate(x, width, expert):
    gates = x[:, width : width + 128].astype(f32)
    lanes = lax.broadcasted_iota(jnp.int32, gates.shape, 1)
    return jnp.sum(jnp.where(lanes == expert, gates, 0.0), axis=1, keepdims=True)


def hidden_lanes(j, size):
    return pl.ds(pl.multiple_of(j * size, size), size)


def scenario_forward_kernel(hidden, own, other, widen, narrow, out_own, out_other, gated):
    half, width = out_own.shape
    total = widen.shape[1]
    size, chunk = min(TILE, total), min(half, max(CHUNK, half // 2))

    def tile(j, _):
        lanes = hidden_lanes(j, size)
        for base, source in ((0, own), (half, other)):
            for at in range(0, half, chunk):
                x = source[at : at + chunk, :]
                gate = chosen_gate(x, width, (j * size) // hidden)
                linear = mm(x[:, :width], widen[:, lanes])
                spot = slice(base + at, base + at + chunk)
                gated[spot, lanes] = (gate * (linear * sigmoid(linear))).astype(bf16)
        return 0

    lax.fori_loop(0, total // size, tile, 0, unroll=True)
    out_own[...] = mm(gated[:half, :], narrow[...]).astype(bf16)
    out_other[...] = mm(gated[half:, :], narrow[...]).astype(bf16)


def put(outs, split, k, b, value, rows=slice(None), lanes=slice(None)):
    out, at, count = (outs[0], b, split) if b < split else (outs[1], b - split, None)
    count = count or outs[1].shape[0] // (outs[0].shape[0] // split)
    out[k * count + at, rows, lanes] = value


def unpack(pieces, turn, xs, gates, xt=None):
    m, packed, _ = pieces[0].shape
    rows = packed - AUX // 2
    for k in range(len(pieces)):
        for b in range(m):
            spot = slice((k * m + b) * rows, (k * m + b + 1) * rows)
            x = pieces[k][b, :rows, :]
            xs[spot, :] = mm(x, turn, 1, 1).astype(bf16)
            gates[spot, :] = mm(side_of(pieces[k][b, rows:, :]), eye(AUX), 0, 0).astype(bf16)
            if xt is not None:
                xt[:, spot] = mm(turn, x, 1, 1).astype(bf16)


def join_rows(top, bottom, out):
    half = top.shape[0]
    out[:half, :] = top[...]
    out[half:, :] = bottom[...]


def join_units_kernel(mine, theirs, out):
    experts, part, _ = mine.shape
    core = own_core()
    for k in range(experts):
        own, other = mine[k], theirs[k]
        out[2 * k * part : (2 * k + 1) * part, :] = jnp.where(core == 0, own, other)
        out[(2 * k + 1) * part : 2 * (k + 1) * part, :] = jnp.where(core == 0, other, own)


def shared_forward_kernel(n, split, gate_rows, gate_count, depth, *refs):
    own, pieces = refs[0], refs[1 : n + 1]
    w1a, w1b, w2, from_own, from_other, *outs, xs, gates, w1, gated = refs[n + 1 :]
    join_rows(w1a, w1b, w1)
    unpack(pieces, turn_matrix(w1.shape[0], depth, own_core()), xs, gates)
    m, packed, _ = pieces[0].shape
    count, rows = n * m, packed - AUX // 2
    capacity = from_own.shape[0] // count
    places = own_place([own], gate_count)
    total = count * rows
    size, chunk = min(TILE, w1.shape[1]), min(total, max(CHUNK, total // 4))

    def tile(j, _):
        lanes = hidden_lanes(j, size)
        picks = spread(j, size, gate_rows)
        for at in range(0, total, chunk):
            spot = slice(at, at + chunk)
            linear = mm(xs[spot, :], w1[:, lanes])
            active = linear * sigmoid(linear)
            gated[spot, lanes] = (mm(gates[spot, :], picks) * active).astype(bf16)
        return 0

    lax.fori_loop(0, w1.shape[1] // size, tile, 0, unroll=True)
    for at in range(0, total, chunk):
        mixed = mm(gated[at : at + chunk, :], w2[...])
        for piece in range(at // rows, (at + chunk) // rows):
            side = side_of(pieces[piece // m][piece % m, rows:, :])
            spot = slice(piece * capacity, (piece + 1) * capacity)
            value = mixed[piece * rows - at : (piece + 1) * rows - at]
            for (owner, _), source in zip(places, (from_own, from_other)):
                value += mm(selector(side, gate_count, owner, capacity), source[spot, :], 0, 0)
            put(outs, split, piece // m, piece % m, value.astype(bf16))


def softmax(v):
    raised = jnp.exp(v - jnp.max(v, axis=1, keepdims=True))
    return raised / jnp.sum(raised, axis=1, keepdims=True)


def head_kernel(count, *refs):
    parts = refs[:count]
    head, mentor, grad, head_part = refs[count:]
    layer = parts[0][...].astype(f32)
    for part in parts[1:]:
        layer = layer + part[...].astype(f32)
    rounded = layer.astype(bf16)
    student = mm(rounded, head[...])
    value = (2.0 * (softmax(student * 0.5) - softmax(mentor[...] * 0.5))).astype(bf16)
    grad[...] = value
    head_part[...] = mm(rounded, value, 0, 0)


def shared_backward_kernel(n, gate_rows, depth, *refs):
    pieces, logits = refs[:n], refs[n : 2 * n]
    head, w1a, w1b, w2 = refs[2 * n : 2 * n + 4]
    dx, mix, keep, sent, keep2, sent2 = refs[2 * n + 4 : 2 * n + 10]
    xp, xpt, gates, w1, os, linear_grad, weighed = refs[2 * n + 10 :]
    core = own_core()
    turn = turn_matrix(w1.shape[0], depth, core)
    join_rows(w1a, w1b, w1)
    unpack(pieces, turn, xp, gates, xpt)
    m, rows, _ = logits[0].shape
    for k in range(n):
        for b in range(m):
            at = (k * m + b) * rows
            os[at : at + rows, :] = mm(logits[k][b], head[...], 1, 1).astype(bf16)
    total = n * m * rows
    size, chunk = weighed.shape[1], min(total, max(CHUNK, total // 4))
    half, part = keep.shape[0], keep2.shape[1]
    mix[...] = jnp.zeros_like(mix)

    def tile(j, _):
        lanes = hidden_lanes(j, size)
        picks = spread(j, size, gate_rows)
        for at in range(0, total, chunk):
            spot = slice(at, at + chunk)
            linear = mm(xp[spot, :], w1[:, lanes])
            hidden = mm(os[spot, :], w2[lanes, :], 1, 1)
            gate = mm(gates[spot, :], picks)
            sig = sigmoid(linear)
            active = linear * sig
            product = hidden * active
            if gate_rows % 128 == 0:
                column = lax.broadcasted_iota(jnp.int32, (chunk, AUX), 1) - j * (size // gate_rows)
                dots = jnp.zeros((chunk, AUX), f32)
                for e in range(size // gate_rows):
                    part_of = product[:, e * gate_rows : (e + 1) * gate_rows]
                    dots = jnp.where(column == e, jnp.sum(part_of, axis=1, keepdims=True), dots)
            else:
                dots = mm(product.astype(bf16), picks, 1, 1)
            mix[spot, :] += dots
            slope = sig + active * (1.0 - sig)
            linear_grad[spot, lanes] = (gate * hidden * slope).astype(bf16)
            weighed[spot, :] = (gate * active).astype(bf16)
        first = mm(xpt[...], linear_grad[:, lanes])
        keep[:, lanes] = first[:half].astype(keep.dtype)
        sent[:, lanes] = first[half:].astype(bf16)
        second = mm(weighed[...], os[...], 0, 0)
        for e in range(size // gate_rows):
            low = second[e * gate_rows : e * gate_rows + part]
            high = second[e * gate_rows + part : (e + 1) * gate_rows]
            k = j * (size // gate_rows) + e
            keep2[k] = jnp.where(core == 0, low, high).astype(keep2.dtype)
            sent2[k] = jnp.where(core == 0, high, low).astype(bf16)
        return 0

    lax.fori_loop(0, w1.shape[1] // size, tile, 0, unroll=True)
    chunk = min(total, 1024)
    for at in range(0, total, chunk):
        spot = slice(at, at + chunk)
        value = mm(linear_grad[spot, :], w1[...], 1, 1).astype(bf16)
        dx[spot, :] = mm(value, turn).astype(bf16)


def scenario_backward_kernel(
    hidden_units, own, other, head, widen, narrow,
    out_own, out_other, dwiden, dnarrow, xs, xt, os, linear_grad, weighed, mix,
):
    half = out_own.shape[0]
    width = narrow.shape[1]
    total = widen.shape[1]
    xs[:half, :] = own[...]
    xs[half:, :] = other[...]
    os[...] = mm(xs[:, width + 128 :], head[...], 1, 1).astype(bf16)
    mix[...] = jnp.zeros_like(mix)
    size, chunk = min(TILE, total), min(2 * half, max(CHUNK, half // 2))
    for at in range(0, 2 * half, chunk):
        xt[:, at : at + chunk] = mm(eye(width), xs[at : at + chunk, :width], 1, 1).astype(bf16)

    def tile(j, _):
        lanes = hidden_lanes(j, size)
        column = (j * size) // hidden_units
        lane = lax.broadcasted_iota(jnp.int32, (chunk, mix.shape[1]), 1)
        for at in range(0, 2 * half, chunk):
            spot = slice(at, at + chunk)
            x = xs[spot, :]
            gate = chosen_gate(x, width, column)
            linear = mm(x[:, :width], widen[:, lanes])
            hidden = mm(os[spot, :], narrow[lanes, :], 1, 1)
            sig = sigmoid(linear)
            active = linear * sig
            product = jnp.sum(hidden * active, axis=1, keepdims=True)
            mix[spot, :] += jnp.where(lane == column, product, 0.0)
            slope = sig + active * (1.0 - sig)
            linear_grad[spot, lanes] = (gate * hidden * slope).astype(bf16)
            weighed[spot, :] = (gate * active).astype(bf16)
        dwiden[:, lanes] = mm(xt[...], linear_grad[:, lanes])
        dnarrow[lanes, :] = mm(weighed[...], os[...], 0, 0)
        return 0

    lax.fori_loop(0, total // size, tile, 0, unroll=True)
    for at, out in ((0, out_own), (half, out_other)):
        out[:, :width] = mm(linear_grad[at : at + half, :], widen[...], 1, 1).astype(bf16)
        out[:, width:] = mix[at : at + half, :].astype(bf16)


def scatter_kernel(n, split, gate_count, *refs):
    pieces = refs[:n]
    dx, mix, from_own, from_other, home, *away, mix_out = refs[n:]
    m, packed, width = pieces[0].shape
    rows = packed - AUX // 2
    capacity = from_own.shape[0] // (n * m)
    places = own_place(pieces, gate_count)
    picks = [gate_picks(first) for _, first in places]
    for k in range(n):
        for b in range(m):
            piece = k * m + b
            spot = slice(piece * capacity, (piece + 1) * capacity)
            full = slice(piece * rows, (piece + 1) * rows)
            side = side_of(pieces[k][b, rows:, :])
            value = dx[full, :].astype(f32)
            dots = mm(eye(AUX), mix[full, :].astype(bf16), 1, 1)
            for (owner, _), pick, source in zip(places, picks, (from_own, from_other)):
                sel = selector(side, gate_count, owner, capacity)
                extra = mm(sel, source[spot, :], 0, 0)
                value += extra[:, :width]
                dots += mm(pick, extra[:, width:].astype(bf16), 1, 1)
            turned = dots.astype(bf16)
            mix_out[piece] = turned
            outs, at, line = (away, k - 1, split) if k else ([home], 0, m)
            put(outs, line, at, b, value.astype(bf16), slice(rows))
            put(outs, line, at, b, turned[: AUX // 2], slice(rows, None), slice(rows))
            put(outs, line, at, b, turned[AUX // 2 :], slice(rows, None), slice(rows, None))


def gate_kernel(n, gate_count, *refs):
    pieces, mix, out = refs[:n], refs[n], refs[n + 1]
    m, packed, _ = pieces[0].shape
    rows = packed - AUX // 2
    live = lax.broadcasted_iota(jnp.int32, (AUX, rows), 0) < gate_count
    count = out.shape[0] // 2
    total = jnp.zeros((count, 2 * out.shape[1]), f32)
    for k in range(n):
        for b in range(m):
            side = side_of(pieces[k][b, rows:, :]).astype(f32)
            dots = mix[k * m + b].astype(f32)
            share = jnp.where(live, side, 0.0)
            share = share / jnp.sum(share, axis=0, keepdims=True)
            score = share * (dots - jnp.sum(share * dots, axis=0, keepdims=True))
            ids = side[gate_count : gate_count + 1, :].astype(jnp.int32)
            wide = score[:gate_count, None, :] * by_scenario(ids, count // gate_count)
            wide = wide.reshape(count, rows).astype(bf16)
            total = total + mm(wide, pieces[k][b, :rows, :])
    out[:count, :] = total[:, : out.shape[1]]
    out[count:, :] = total[:, out.shape[1] :]


def final_kernel(count, gate_count, *refs):
    parts = refs[:count]
    feats, sid, probs, gate, out = refs[count:]
    rows = feats.shape[0]
    total = parts[0][...].astype(f32)
    for part in parts[1:]:
        total = total + part[...].astype(f32)
    tail = total[rows:]
    half = tail.shape[1] // 2
    dots = jnp.concatenate([tail[:, :half], tail[:, half:]], axis=0)
    share = probs[...]
    live = lax.broadcasted_iota(jnp.int32, (AUX, rows), 0) < gate_count
    dots = jnp.where(live, dots, 0.0)
    score = share * (dots - jnp.sum(share * dots, axis=0, keepdims=True))
    score = score.astype(bf16).astype(f32)[:gate_count]
    wide = score[:, None, :] * by_scenario(sid[...], gate.shape[0] // gate_count)
    wide = wide.reshape(gate.shape[0], rows).astype(bf16)
    out[...] = (total[:rows] + mm(wide, gate[...], 0, 0)).astype(bf16)


def expand_grad_kernel(pieces, out):
    count, _, hidden = out.shape
    chips = pieces.shape[0]
    lanes = hidden // chips
    for k in range(count):
        for chip in range(chips):
            out[k, :, chip * lanes : (chip + 1) * lanes] = pieces[
                chip, :, k * lanes : (k + 1) * lanes
            ].astype(f32)


def body(
    features,
    scenario_id,
    scenario_pads,
    device_slot,
    mentor,
    gate_weight,
    expand,
    reduce,
    scenario_widen,
    scenario_narrow,
    head,
):
    rows, width = features.shape
    devices = lax.axis_size(AXIS)
    chips = devices // 2
    near = 2 ** ((chips.bit_length() - 1) // 2)
    far = chips // near
    n, m = near, far
    shared, depth, hidden = expand.shape
    lanes = hidden // chips
    scenarios, _, gates = gate_weight.shape
    capacity = rows // 4
    slot_width = scenario_widen.shape[2]
    classes = head.shape[1]
    all_rows = chips * rows
    assert gates + 6 <= AUX and rows == 128
    slots = chips * capacity
    hidden_chip = shared * lanes
    groups = [[2 * r + c for r in range(chips)] for c in range(2)]

    def send(value, mask):
        return lax.ppermute(value, AXIS, [(i, i ^ mask) for i in range(devices)])

    def gather(value):
        column = [value] + [send(value, 2 * near * b) for b in range(1, far)]
        stacked = jnp.stack(column)
        return [stacked] + [send(stacked, 2 * a) for a in range(1, near)]

    def total_of(value, masks):
        for mask in masks:
            half = value.astype(bf16)
            value = half.astype(f32) + send(half, mask).astype(f32)
        return value

    sid = scenario_id.reshape(1, rows)
    gate = jnp.transpose(gate_weight, (2, 0, 1)).reshape(gates * scenarios, width)
    widen, narrow = scenario_widen[0], scenario_narrow[0]
    tiled = lanes % 128 == 0 and depth % 16 == 0
    if not tiled:
        expand = expand.reshape(shared, depth, chips, lanes).transpose(2, 1, 0, 3)
        expand = expand.reshape(chips, depth, hidden_chip)

    pack_rows = rows + AUX // 2
    pack, probs = call(
        functools.partial(prep_kernel, shared, hidden, slot_width),
        [struct((pack_rows, width), bf16), struct((AUX, rows), f32)],
        [scenario_pads, device_slot, features, sid, gate],
        [SCALARS] * 2 + [None] * 3,
        [pltpu.VMEM((AUX, rows), f32)],
        limit=FIRST,
    )
    (pieces,) = call(
        functools.partial(tile_kernel, tiled),
        [struct((chips, depth, hidden_chip), bf16)],
        [expand],
        limit=SMALL,
    )
    column = [pack] + [send(pack, 2 * near * b) for b in range(1, far)]
    column, pieces = lax.optimization_barrier((column, pieces))
    stacked = jnp.stack(column)
    got = [stacked] + [send(stacked, 2 * a) for a in range(1, near)]
    (w2,) = call(
        join_units_kernel,
        [struct((hidden_chip, width), bf16)],
        [reduce, send(reduce, 1)],
        limit=SMALL,
    )
    w1a = lax.all_to_all(
        pieces, AXIS, split_axis=0, concat_axis=0, tiled=True, axis_index_groups=groups
    ).reshape(width // 2, hidden_chip)
    def compact(pieces, values):
        count = len(pieces) * far * capacity
        out_width = width + 128 + (classes if values else 0)
        return call(
            functools.partial(compact_kernel, len(pieces), gates, capacity),
            [struct((count, out_width), bf16)] * 2,
            [got[0], *pieces, *values],
            limit=SMALL,
        )

    def scenario_forward(pieces):
        count = len(pieces) * far * capacity
        x_own, x_send = compact(pieces, [])
        out_own, out_send = call(
            functools.partial(scenario_forward_kernel, hidden),
            [struct((count, width), bf16)] * 2,
            [x_own, send(x_send, 1), widen, narrow],
            scratch=[pltpu.VMEM((2 * count, slot_width), bf16)],
            limit=SMALL,
        )
        return out_own, send(out_send, 1)

    mixing_home = scenario_forward(got[:1])
    got[1], mixing_home, w1a, w2 = lax.optimization_barrier((got[1], mixing_home, w1a, w2))
    mixing_away = scenario_forward(got[1:])
    w1b = send(w1a, 1)
    weights = [w1a, w1b, w2]
    weight_scratch = [pltpu.VMEM((width, hidden_chip), bf16)]

    def forward(pieces, mixing, lines):
        count = len(pieces) * far
        return call(
            functools.partial(shared_forward_kernel, len(pieces), lines[0], lanes, gates, depth),
            [struct((len(pieces) * line, rows, width), bf16) for line in lines],
            [got[0], *pieces, *weights, *mixing],
            scratch=[
                pltpu.VMEM((count * rows, width), bf16),
                pltpu.VMEM((count * rows, AUX), bf16),
                *weight_scratch,
                pltpu.VMEM((count * rows, hidden_chip), bf16),
            ],
            limit=BIG,
        )

    split = far // 2
    lines = (split, far - split)
    away = forward(got[1:], mixing_away, lines)
    (home,) = forward(got[:1], mixing_home, (far,))

    def along_near(home, away):
        count = home.shape[0]
        total = home.astype(f32)
        for a in range(1, near):
            total = total + send(away[(a - 1) * count : a * count], 2 * a).astype(f32)
        return total.astype(bf16)

    def along_far(low, high):
        column = [low[b] for b in range(split)] + [high[b] for b in range(far - split)]
        return [column[0]] + [send(column[b], 2 * near * b) for b in range(1, far)]

    high = along_near(home[split:], away[1])
    low = along_near(home[:split], away[0])
    layer_parts = along_far(low, high)
    logit_grad, head_part = call(
        functools.partial(head_kernel, len(layer_parts)),
        [struct((rows, classes), bf16), struct((width, classes), f32)],
        [*layer_parts, head, mentor],
        limit=8,
    )
    logits = gather(logit_grad)
    masks = [2**i for i in range(devices.bit_length() - 2, 0, -1)]
    head_part = total_of(head_part + send(head_part, 1), masks[:1])
    logits[0], head_part = lax.optimization_barrier((logits[0], head_part))

    x_own, x_send = compact(got, logits)
    logits[0], x_send = lax.optimization_barrier((logits[0], x_send))
    x_other = send(x_send, 1)
    dx, mix, dw1_keep, dw1_send, dw2_keep, dw2_send = call(
        functools.partial(shared_backward_kernel, n, lanes, depth),
        [
            struct((all_rows, width), bf16),
            struct((all_rows, AUX), f32),
            struct((width // 2, hidden_chip), bf16),
            struct((width // 2, hidden_chip), bf16),
            struct((shared, lanes // 2, width), bf16),
            struct((shared, lanes // 2, width), bf16),
        ],
        [*got, *logits, head, *weights],
        scratch=[
            pltpu.VMEM((all_rows, width), bf16),
            pltpu.VMEM((width, all_rows), bf16),
            pltpu.VMEM((all_rows, AUX), bf16),
            *weight_scratch,
            pltpu.VMEM((all_rows, width), bf16),
            pltpu.VMEM((all_rows, hidden_chip), bf16),
            pltpu.VMEM((all_rows, min(256, hidden_chip)), bf16),
        ],
        limit=BIG,
    )
    dw1 = (dw1_keep.astype(f32) + send(dw1_send, 1).astype(f32)).astype(bf16)
    dw1, x_own = lax.optimization_barrier((dw1, x_own))
    dw1 = lax.all_to_all(
        dw1.reshape(chips, depth, hidden_chip),
        AXIS, split_axis=0, concat_axis=0, tiled=True, axis_index_groups=groups,
    )
    dx_own, dx_send, widen_grad, narrow_grad = call(
        functools.partial(scenario_backward_kernel, hidden),
        [struct((slots, width + 128), bf16)] * 2
        + [struct((width, slot_width), f32), struct((slot_width, width), f32)],
        [x_own, x_other, head, widen, narrow],
        None,
        [
            pltpu.VMEM((2 * slots, width + 128 + classes), bf16),
            pltpu.VMEM((width, 2 * slots), bf16),
            pltpu.VMEM((2 * slots, width), bf16),
            pltpu.VMEM((2 * slots, slot_width), bf16),
            pltpu.VMEM((2 * slots, min(TILE, slot_width)), bf16),
            pltpu.VMEM((2 * slots, 128), f32),
        ],
        limit=BIG,
    )
    dx_other = send(dx_send, 1)
    dw2_came = send(dw2_send, 1)
    grad_home, low, high, mix = call(
        functools.partial(scatter_kernel, n, split, gates),
        [
            struct((far, pack_rows, width), bf16),
            *[struct(((near - 1) * line, pack_rows, width), bf16) for line in lines],
            struct((chips, AUX, rows), bf16),
        ],
        [*got, dx, mix, dx_own, dx_other],
        limit=SMALL,
    )
    (gate_part,) = call(
        functools.partial(gate_kernel, n, gates),
        [struct((2 * gates * scenarios, width // 2), f32)],
        [*got, mix],
        limit=SMALL,
    )
    gate_part = gate_part + send(gate_part, 1)
    count = gate_part.shape[0]
    joined = classes == width // 2
    low, high, gate_part, dw1 = lax.optimization_barrier((low, high, gate_part, dw1))
    high = along_near(grad_home[split:], high)
    low = along_near(grad_home[:split], low)
    low, dw2_keep = lax.optimization_barrier((low, dw2_keep))
    grad_parts = along_far(low, high)
    reduce_grad = dw2_keep.astype(f32) + dw2_came.astype(f32)
    gate_part = total_of(gate_part, masks[:1])
    if joined:
        value = total_of(jnp.concatenate([gate_part, head_part]), masks[1:-1])
        kept = value.astype(bf16)
        came = send(kept, masks[-1])
        gate_total = kept[:count].astype(f32) + came[:count].astype(f32)
        head_total = kept[count:].astype(f32) + came[count:].astype(f32)
    else:
        gate_total = total_of(gate_part, masks[1:])
        head_total = total_of(head_part, masks[1:])
    halves = [gate_total[: count // 2], gate_total[count // 2 :]]
    gate_total = jnp.concatenate(halves, axis=1).reshape(gates, scenarios, width)
    gate_total = jnp.transpose(gate_total, (1, 2, 0))
    if tiled:
        (expand_grad,) = call(
            expand_grad_kernel, [struct((shared, depth, hidden), f32)], [dw1], limit=8
        )
    else:
        expand_grad = dw1.reshape(chips, depth, shared, lanes).transpose(2, 1, 0, 3)
        expand_grad = expand_grad.reshape(shared, depth, hidden).astype(f32)

    grad_parts, gate_total, head_total = lax.optimization_barrier(
        (grad_parts, gate_total, head_total)
    )
    (feature_grad,) = call(
        functools.partial(final_kernel, len(grad_parts), gates),
        [struct((rows, width), bf16)],
        [*grad_parts, features, sid, probs, gate],
        limit=8,
    )
    return (
        feature_grad,
        expand_grad,
        reduce_grad,
        widen_grad[None],
        narrow_grad[None],
        gate_total,
        head_total,
    )


def solution(mesh):
    placed = (
        P(("groups", "expert"), None),
        P(("groups", "expert")),
        P("groups"),
        P(),
        P(("groups", "expert"), None),
        P(),
        P(None, "expert", None),
        P(None, "expert", None),
        P("expert", None, None),
        P("expert", None, None),
        P(),
    )
    return jax.shard_map(
        body,
        mesh=mesh,
        in_specs=placed,
        out_specs=(
            P(("groups", "expert"), None),
            P("groups", "expert", None),
            P("groups", "expert", None),
            P(("groups", "expert"), None, None),
            P(("groups", "expert"), None, None),
            P("groups", None, None),
            P("groups", None),
        ),
        check_vma=False,
    )
```

```python
import functools

import jax
import jax.numpy as jnp
from jax import lax
from jax.experimental import pallas as pl
from jax.experimental.pallas import tpu as pltpu
from jax.sharding import PartitionSpec as P

AXIS = "expert"
TILE = 512
AUX = 32
bf16 = jnp.bfloat16
f32 = jnp.float32
CHUNK = 256
FIRST, SMALL, BIG = 60, 16, 32
COST = 100000


def mm(left, right, left_dim=1, right_dim=0):
    return lax.dot_general(
        left, right, (((left_dim,), (right_dim,)), ((), ())), preferred_element_type=f32
    )


def call(kernel, out_shapes, operands, in_specs=None, scratch=(), limit=48):
    specs = in_specs or [None] * len(operands)
    specs = [pl.BlockSpec(memory_space=pltpu.VMEM) if s is None else s for s in specs]
    return pl.pallas_call(
        kernel,
        out_shape=out_shapes,
        in_specs=specs,
        out_specs=[pl.BlockSpec(memory_space=pltpu.VMEM) for _ in out_shapes],
        scratch_shapes=list(scratch),
        compiler_params=pltpu.CompilerParams(vmem_limit_bytes=limit * 1024 * 1024),
        cost_estimate=pl.CostEstimate(flops=COST, bytes_accessed=COST, transcendentals=0),
    )(*operands)


SCALARS = pl.BlockSpec(memory_space=pltpu.SMEM)


def own_core():
    return lax.rem(lax.axis_index(AXIS), 2)


def struct(shape, kind):
    return jax.ShapeDtypeStruct(shape, kind)


def sigmoid(v):
    return 0.5 * (1.0 + jnp.tanh(0.5 * v))


def eye(size):
    rows = lax.broadcasted_iota(jnp.int32, (size, size), 0)
    cols = lax.broadcasted_iota(jnp.int32, (size, size), 1)
    return (rows == cols).astype(f32).astype(bf16)


def spread(tile, size, expert_lanes):
    rows = lax.broadcasted_iota(jnp.int32, (AUX, size), 0)
    lanes = lax.broadcasted_iota(jnp.int32, (AUX, size), 1) + tile * size
    first = rows * expert_lanes
    return ((lanes >= first) & (lanes < first + expert_lanes)).astype(f32).astype(bf16)


def turn_matrix(size, depth, core):
    place = lax.broadcasted_iota(jnp.int32, (size, size), 0)
    column = lax.broadcasted_iota(jnp.int32, (size, size), 1)
    half = size // 2
    other = place // half
    place = place - other * half
    chip = place // depth
    which = jnp.where(core == 0, other, 1 - other)
    return (column == (chip * 2 + which) * depth + (place - chip * depth)).astype(f32).astype(bf16)


def side_of(piece):
    half = piece.shape[1] // 2
    return jnp.concatenate([piece[:, :half], piece[:, half:]], axis=0)


def selector(side, gate_count, owner, capacity):
    wide = side.astype(f32)
    which = wide[gate_count : gate_count + 1, :]
    slot = wide[gate_count + 1 : gate_count + 2, :]
    ranks = lax.broadcasted_iota(jnp.int32, (capacity, side.shape[1]), 0).astype(f32)
    hit = (ranks == slot) & (which == owner)
    return hit.astype(f32).astype(bf16)


def placement(own_side, gate_count):
    wide = own_side.astype(f32)
    rows = [wide[gate_count + 2 + i : gate_count + 3 + i, :] for i in range(4)]
    return (rows[0], rows[1]), (rows[2], rows[3])


def gate_picks(first):
    shape = (AUX, first.shape[1])
    rows = lax.broadcasted_iota(jnp.int32, shape, 0)
    lanes = lax.broadcasted_iota(jnp.int32, shape, 1)
    return ((rows - lanes).astype(f32) == first).astype(f32).astype(bf16)


def by_scenario(ids, scenarios):
    labels = lax.broadcasted_iota(jnp.int32, (scenarios, ids.shape[1]), 0)
    return (labels == ids).astype(f32)[None]


def prep_kernel(shared, hidden, slot_width, pads, slots, feats, sid, gate, pack, probs, scr):
    scenarios = pads.shape[0]
    gate_count = gate.shape[0] // scenarios
    rows = feats.shape[0]
    x = feats[...]
    ids = sid[...]
    scr[...] = jnp.zeros_like(scr)
    pad = jnp.zeros((1, rows), f32)
    for s in range(scenarios):
        pad = pad + jnp.where(ids == s, pads[s].astype(f32), 0.0)
    logits = mm(gate[...], x, 1, 1).reshape(gate_count, scenarios, rows)
    own = jnp.sum(logits * by_scenario(ids, scenarios), axis=1)
    top = jnp.max(own, axis=0, keepdims=True)
    raised = jnp.exp(own - top)
    scr[:gate_count, :] = raised / jnp.sum(raised, axis=0, keepdims=True)
    probs[...] = scr[...]
    labels = lax.broadcasted_iota(jnp.int32, (AUX, rows), 0)
    member = (ids == labels).astype(f32)
    earlier = (
        lax.broadcasted_iota(jnp.int32, (rows, rows), 0)
        < lax.broadcasted_iota(jnp.int32, (rows, rows), 1)
    ).astype(f32).astype(bf16)
    rank = jnp.sum(mm(member.astype(bf16), earlier) * member, axis=0, keepdims=True)
    slot = jnp.where(rank < pad, rank, -1.0)
    scr[gate_count : gate_count + 1, :] = ids.astype(f32)
    scr[gate_count + 1 : gate_count + 2, :] = slot
    index = lax.axis_index(AXIS)
    group = slots.shape[0] // scenarios
    for i, device in enumerate((index, index + 1 - 2 * lax.rem(index, 2))):
        owned = slots[device]
        first = shared + lax.rem(owned, group) * slot_width // hidden
        for j, value in enumerate((owned // group, first)):
            at = gate_count + 2 + 2 * i + j
            scr[at : at + 1, :] = jnp.zeros((1, rows), f32) + value.astype(f32)
    side = scr[...].astype(bf16)
    pack[:rows, :] = x
    pack[rows:, :rows] = side[: AUX // 2]
    pack[rows:, rows:] = side[AUX // 2 :]


def tile_kernel(tiled, expand, pieces):
    if tiled:
        chips, _, total = pieces.shape
        count = expand.shape[0]
        lanes = total // count
        for k in range(count):
            for chip in range(chips):
                pieces[chip, :, k * lanes : (k + 1) * lanes] = expand[
                    k, :, chip * lanes : (chip + 1) * lanes
                ]
    else:
        pieces[...] = expand[...]


def own_place(pieces, gate_count):
    return placement(side_of(pieces[0][0, pieces[0].shape[1] - AUX // 2 :, :]), gate_count)


def compact_kernel(n, gate_count, capacity, *refs):
    own, pieces, logits, outs = refs[0], refs[1 : n + 1], refs[n + 1 : -2], refs[-2:]
    m = pieces[0].shape[0]
    rows = pieces[0].shape[1] - AUX // 2
    width = pieces[0].shape[2]
    places = own_place([own], gate_count)
    for k in range(n):
        for b in range(m):
            x = pieces[k][b, :rows, :]
            side = side_of(pieces[k][b, rows:, :])
            spot = slice((k * m + b) * capacity, (k * m + b + 1) * capacity)
            for (owner, first), out in zip(places, outs):
                sel = selector(side, gate_count, owner, capacity)
                out[spot, :width] = mm(sel, x).astype(bf16)
                gates = mm(sel, side, 1, 1).astype(bf16)
                out[spot, width : width + rows] = mm(gates, gate_picks(first)).astype(bf16)
                if logits:
                    out[spot, width + rows :] = mm(sel, logits[k][b]).astype(bf16)


def chosen_gate(x, width, expert):
    gates = x[:, width : width + 128].astype(f32)
    lanes = lax.broadcasted_iota(jnp.int32, gates.shape, 1)
    return jnp.sum(jnp.where(lanes == expert, gates, 0.0), axis=1, keepdims=True)


def hidden_lanes(j, size):
    return pl.ds(pl.multiple_of(j * size, size), size)


def scenario_forward_kernel(hidden, own, other, widen, narrow, out_own, out_other, gated):
    half, width = out_own.shape
    total = widen.shape[1]
    size, chunk = min(TILE, total), min(half, max(CHUNK, half // 2))

    def tile(j, _):
        lanes = hidden_lanes(j, size)
        for base, source in ((0, own), (half, other)):
            for at in range(0, half, chunk):
                x = source[at : at + chunk, :]
                gate = chosen_gate(x, width, (j * size) // hidden)
                linear = mm(x[:, :width], widen[:, lanes])
                spot = slice(base + at, base + at + chunk)
                gated[spot, lanes] = (gate * (linear * sigmoid(linear))).astype(bf16)
        return 0

    lax.fori_loop(0, total // size, tile, 0, unroll=True)
    out_own[...] = mm(gated[:half, :], narrow[...]).astype(bf16)
    out_other[...] = mm(gated[half:, :], narrow[...]).astype(bf16)


def put(outs, split, k, b, value, rows=slice(None), lanes=slice(None)):
    out, at, count = (outs[0], b, split) if b < split else (outs[1], b - split, None)
    count = count or outs[1].shape[0] // (outs[0].shape[0] // split)
    out[k * count + at, rows, lanes] = value


def unpack(pieces, turn, xs, gates, xt=None):
    m, packed, _ = pieces[0].shape
    rows = packed - AUX // 2
    for k in range(len(pieces)):
        for b in range(m):
            spot = slice((k * m + b) * rows, (k * m + b + 1) * rows)
            x = pieces[k][b, :rows, :]
            xs[spot, :] = mm(x, turn, 1, 1).astype(bf16)
            gates[spot, :] = mm(side_of(pieces[k][b, rows:, :]), eye(AUX), 0, 0).astype(bf16)
            if xt is not None:
                xt[:, spot] = mm(turn, x, 1, 1).astype(bf16)


def join_rows(top, bottom, out):
    half = top.shape[0]
    out[:half, :] = top[...]
    out[half:, :] = bottom[...]


def join_units_kernel(mine, theirs, out):
    experts, part, _ = mine.shape
    core = own_core()
    for k in range(experts):
        own, other = mine[k], theirs[k]
        out[2 * k * part : (2 * k + 1) * part, :] = jnp.where(core == 0, own, other)
        out[(2 * k + 1) * part : 2 * (k + 1) * part, :] = jnp.where(core == 0, other, own)


def shared_forward_kernel(n, split, gate_rows, gate_count, depth, *refs):
    own, pieces = refs[0], refs[1 : n + 1]
    w1a, w1b, w2, from_own, from_other, *outs, xs, gates, w1, gated = refs[n + 1 :]
    join_rows(w1a, w1b, w1)
    unpack(pieces, turn_matrix(w1.shape[0], depth, own_core()), xs, gates)
    m, packed, _ = pieces[0].shape
    count, rows = n * m, packed - AUX // 2
    capacity = from_own.shape[0] // count
    places = own_place([own], gate_count)
    total = count * rows
    size, chunk = min(TILE, w1.shape[1]), min(total, max(CHUNK, total // 4))

    def tile(j, _):
        lanes = hidden_lanes(j, size)
        picks = spread(j, size, gate_rows)
        for at in range(0, total, chunk):
            spot = slice(at, at + chunk)
            linear = mm(xs[spot, :], w1[:, lanes])
            active = linear * sigmoid(linear)
            gated[spot, lanes] = (mm(gates[spot, :], picks) * active).astype(bf16)
        return 0

    lax.fori_loop(0, w1.shape[1] // size, tile, 0, unroll=True)
    for at in range(0, total, chunk):
        mixed = mm(gated[at : at + chunk, :], w2[...])
        for piece in range(at // rows, (at + chunk) // rows):
            side = side_of(pieces[piece // m][piece % m, rows:, :])
            spot = slice(piece * capacity, (piece + 1) * capacity)
            value = mixed[piece * rows - at : (piece + 1) * rows - at]
            for (owner, _), source in zip(places, (from_own, from_other)):
                value += mm(selector(side, gate_count, owner, capacity), source[spot, :], 0, 0)
            put(outs, split, piece // m, piece % m, value.astype(bf16))


def softmax(v):
    raised = jnp.exp(v - jnp.max(v, axis=1, keepdims=True))
    return raised / jnp.sum(raised, axis=1, keepdims=True)


def head_kernel(count, *refs):
    parts = refs[:count]
    head, mentor, grad, head_part = refs[count:]
    layer = parts[0][...].astype(f32)
    for part in parts[1:]:
        layer = layer + part[...].astype(f32)
    rounded = layer.astype(bf16)
    student = mm(rounded, head[...])
    value = (2.0 * (softmax(student * 0.5) - softmax(mentor[...] * 0.5))).astype(bf16)
    grad[...] = value
    head_part[...] = mm(rounded, value, 0, 0)


def shared_backward_kernel(n, gate_rows, depth, *refs):
    pieces, logits = refs[:n], refs[n : 2 * n]
    head, w1a, w1b, w2 = refs[2 * n : 2 * n + 4]
    dx, mix, keep, sent, keep2, sent2 = refs[2 * n + 4 : 2 * n + 10]
    xp, xpt, gates, w1, os, linear_grad, weighed = refs[2 * n + 10 :]
    core = own_core()
    turn = turn_matrix(w1.shape[0], depth, core)
    join_rows(w1a, w1b, w1)
    unpack(pieces, turn, xp, gates, xpt)
    m, rows, _ = logits[0].shape
    for k in range(n):
        for b in range(m):
            at = (k * m + b) * rows
            os[at : at + rows, :] = mm(logits[k][b], head[...], 1, 1).astype(bf16)
    total = n * m * rows
    size, chunk = weighed.shape[1], min(total, max(CHUNK, total // 4))
    half, part = keep.shape[0], keep2.shape[1]
    mix[...] = jnp.zeros_like(mix)

    def tile(j, _):
        lanes = hidden_lanes(j, size)
        picks = spread(j, size, gate_rows)
        for at in range(0, total, chunk):
            spot = slice(at, at + chunk)
            linear = mm(xp[spot, :], w1[:, lanes])
            hidden = mm(os[spot, :], w2[lanes, :], 1, 1)
            gate = mm(gates[spot, :], picks)
            sig = sigmoid(linear)
            active = linear * sig
            product = hidden * active
            if gate_rows % 128 == 0:
                column = lax.broadcasted_iota(jnp.int32, (chunk, AUX), 1) - j * (size // gate_rows)
                dots = jnp.zeros((chunk, AUX), f32)
                for e in range(size // gate_rows):
                    part_of = product[:, e * gate_rows : (e + 1) * gate_rows]
                    dots = jnp.where(column == e, jnp.sum(part_of, axis=1, keepdims=True), dots)
            else:
                dots = mm(product.astype(bf16), picks, 1, 1)
            mix[spot, :] += dots
            slope = sig + active * (1.0 - sig)
            linear_grad[spot, lanes] = (gate * hidden * slope).astype(bf16)
            weighed[spot, :] = (gate * active).astype(bf16)
        first = mm(xpt[...], linear_grad[:, lanes])
        keep[:, lanes] = first[:half].astype(keep.dtype)
        sent[:, lanes] = first[half:].astype(bf16)
        second = mm(weighed[...], os[...], 0, 0)
        for e in range(size // gate_rows):
            low = second[e * gate_rows : e * gate_rows + part]
            high = second[e * gate_rows + part : (e + 1) * gate_rows]
            k = j * (size // gate_rows) + e
            keep2[k] = jnp.where(core == 0, low, high).astype(keep2.dtype)
            sent2[k] = jnp.where(core == 0, high, low).astype(bf16)
        return 0

    lax.fori_loop(0, w1.shape[1] // size, tile, 0, unroll=True)
    chunk = min(total, 1024)
    for at in range(0, total, chunk):
        spot = slice(at, at + chunk)
        value = mm(linear_grad[spot, :], w1[...], 1, 1).astype(bf16)
        dx[spot, :] = mm(value, turn).astype(bf16)


def scenario_backward_kernel(
    hidden_units, own, other, head, widen, narrow,
    out_own, out_other, dwiden, dnarrow, xs, xt, os, linear_grad, weighed, mix,
):
    half = out_own.shape[0]
    width = narrow.shape[1]
    total = widen.shape[1]
    xs[:half, :] = own[...]
    xs[half:, :] = other[...]
    os[...] = mm(xs[:, width + 128 :], head[...], 1, 1).astype(bf16)
    mix[...] = jnp.zeros_like(mix)
    size, chunk = min(TILE, total), min(2 * half, max(CHUNK, half // 2))
    for at in range(0, 2 * half, chunk):
        xt[:, at : at + chunk] = mm(eye(width), xs[at : at + chunk, :width], 1, 1).astype(bf16)

    def tile(j, _):
        lanes = hidden_lanes(j, size)
        column = (j * size) // hidden_units
        lane = lax.broadcasted_iota(jnp.int32, (chunk, mix.shape[1]), 1)
        for at in range(0, 2 * half, chunk):
            spot = slice(at, at + chunk)
            x = xs[spot, :]
            gate = chosen_gate(x, width, column)
            linear = mm(x[:, :width], widen[:, lanes])
            hidden = mm(os[spot, :], narrow[lanes, :], 1, 1)
            sig = sigmoid(linear)
            active = linear * sig
            product = jnp.sum(hidden * active, axis=1, keepdims=True)
            mix[spot, :] += jnp.where(lane == column, product, 0.0)
            slope = sig + active * (1.0 - sig)
            linear_grad[spot, lanes] = (gate * hidden * slope).astype(bf16)
            weighed[spot, :] = (gate * active).astype(bf16)
        dwiden[:, lanes] = mm(xt[...], linear_grad[:, lanes])
        dnarrow[lanes, :] = mm(weighed[...], os[...], 0, 0)
        return 0

    lax.fori_loop(0, total // size, tile, 0, unroll=True)
    for at, out in ((0, out_own), (half, out_other)):
        out[:, :width] = mm(linear_grad[at : at + half, :], widen[...], 1, 1).astype(bf16)
        out[:, width:] = mix[at : at + half, :].astype(bf16)


def scatter_kernel(n, split, gate_count, *refs):
    pieces = refs[:n]
    dx, mix, from_own, from_other, home, *away, mix_out = refs[n:]
    m, packed, width = pieces[0].shape
    rows = packed - AUX // 2
    capacity = from_own.shape[0] // (n * m)
    places = own_place(pieces, gate_count)
    picks = [gate_picks(first) for _, first in places]
    for k in range(n):
        for b in range(m):
            piece = k * m + b
            spot = slice(piece * capacity, (piece + 1) * capacity)
            full = slice(piece * rows, (piece + 1) * rows)
            side = side_of(pieces[k][b, rows:, :])
            value = dx[full, :].astype(f32)
            dots = mm(eye(AUX), mix[full, :].astype(bf16), 1, 1)
            for (owner, _), pick, source in zip(places, picks, (from_own, from_other)):
                sel = selector(side, gate_count, owner, capacity)
                extra = mm(sel, source[spot, :], 0, 0)
                value += extra[:, :width]
                dots += mm(pick, extra[:, width:].astype(bf16), 1, 1)
            turned = dots.astype(bf16)
            mix_out[piece] = turned
            outs, at, line = (away, k - 1, split) if k else ([home], 0, m)
            put(outs, line, at, b, value.astype(bf16), slice(rows))
            put(outs, line, at, b, turned[: AUX // 2], slice(rows, None), slice(rows))
            put(outs, line, at, b, turned[AUX // 2 :], slice(rows, None), slice(rows, None))


def gate_kernel(n, gate_count, *refs):
    pieces, mix, out = refs[:n], refs[n], refs[n + 1]
    m, packed, _ = pieces[0].shape
    rows = packed - AUX // 2
    live = lax.broadcasted_iota(jnp.int32, (AUX, rows), 0) < gate_count
    count = out.shape[0] // 2
    total = jnp.zeros((count, 2 * out.shape[1]), f32)
    for k in range(n):
        for b in range(m):
            side = side_of(pieces[k][b, rows:, :]).astype(f32)
            dots = mix[k * m + b].astype(f32)
            share = jnp.where(live, side, 0.0)
            share = share / jnp.sum(share, axis=0, keepdims=True)
            score = share * (dots - jnp.sum(share * dots, axis=0, keepdims=True))
            ids = side[gate_count : gate_count + 1, :].astype(jnp.int32)
            wide = score[:gate_count, None, :] * by_scenario(ids, count // gate_count)
            wide = wide.reshape(count, rows).astype(bf16)
            total = total + mm(wide, pieces[k][b, :rows, :])
    out[:count, :] = total[:, : out.shape[1]]
    out[count:, :] = total[:, out.shape[1] :]


def final_kernel(count, gate_count, *refs):
    parts = refs[:count]
    feats, sid, probs, gate, out = refs[count:]
    rows = feats.shape[0]
    total = parts[0][...].astype(f32)
    for part in parts[1:]:
        total = total + part[...].astype(f32)
    tail = total[rows:]
    half = tail.shape[1] // 2
    dots = jnp.concatenate([tail[:, :half], tail[:, half:]], axis=0)
    share = probs[...]
    live = lax.broadcasted_iota(jnp.int32, (AUX, rows), 0) < gate_count
    dots = jnp.where(live, dots, 0.0)
    score = share * (dots - jnp.sum(share * dots, axis=0, keepdims=True))
    score = score.astype(bf16).astype(f32)[:gate_count]
    wide = score[:, None, :] * by_scenario(sid[...], gate.shape[0] // gate_count)
    wide = wide.reshape(gate.shape[0], rows).astype(bf16)
    out[...] = (total[:rows] + mm(wide, gate[...], 0, 0)).astype(bf16)


def expand_grad_kernel(pieces, out):
    count, _, hidden = out.shape
    chips = pieces.shape[0]
    lanes = hidden // chips
    for k in range(count):
        for chip in range(chips):
            out[k, :, chip * lanes : (chip + 1) * lanes] = pieces[
                chip, :, k * lanes : (k + 1) * lanes
            ].astype(f32)


def body(
    features,
    scenario_id,
    scenario_pads,
    device_slot,
    mentor,
    gate_weight,
    expand,
    reduce,
    scenario_widen,
    scenario_narrow,
    head,
):
    rows, width = features.shape
    devices = lax.axis_size(AXIS)
    chips = devices // 2
    near = 2 ** ((chips.bit_length() - 1) // 2)
    far = chips // near
    n, m = near, far
    shared, depth, hidden = expand.shape
    lanes = hidden // chips
    scenarios, _, gates = gate_weight.shape
    capacity = rows // 4
    slot_width = scenario_widen.shape[2]
    classes = head.shape[1]
    all_rows = chips * rows
    assert gates + 6 <= AUX and rows == 128
    slots = chips * capacity
    hidden_chip = shared * lanes
    groups = [[2 * r + c for r in range(chips)] for c in range(2)]

    def send(value, mask):
        return lax.ppermute(value, AXIS, [(i, i ^ mask) for i in range(devices)])

    def gather(value):
        column = [value] + [send(value, 2 * near * b) for b in range(1, far)]
        stacked = jnp.stack(column)
        return [stacked] + [send(stacked, 2 * a) for a in range(1, near)]

    def total_of(value, masks):
        for mask in masks:
            half = value.astype(bf16)
            value = half.astype(f32) + send(half, mask).astype(f32)
        return value

    sid = scenario_id.reshape(1, rows)
    gate = jnp.transpose(gate_weight, (2, 0, 1)).reshape(gates * scenarios, width)
    widen, narrow = scenario_widen[0], scenario_narrow[0]
    tiled = lanes % 128 == 0 and depth % 16 == 0
    if not tiled:
        expand = expand.reshape(shared, depth, chips, lanes).transpose(2, 1, 0, 3)
        expand = expand.reshape(chips, depth, hidden_chip)

    pack_rows = rows + AUX // 2
    pack, probs = call(
        functools.partial(prep_kernel, shared, hidden, slot_width),
        [struct((pack_rows, width), bf16), struct((AUX, rows), f32)],
        [scenario_pads, device_slot, features, sid, gate],
        [SCALARS] * 2 + [None] * 3,
        [pltpu.VMEM((AUX, rows), f32)],
        limit=FIRST,
    )
    (pieces,) = call(
        functools.partial(tile_kernel, tiled),
        [struct((chips, depth, hidden_chip), bf16)],
        [expand],
        limit=SMALL,
    )
    column = [pack] + [send(pack, 2 * near * b) for b in range(1, far)]
    column, pieces = lax.optimization_barrier((column, pieces))
    stacked = jnp.stack(column)
    got = [stacked] + [send(stacked, 2 * a) for a in range(1, near)]
    reduce_other = send(reduce, 1)
    w1a = lax.all_to_all(
        pieces, AXIS, split_axis=0, concat_axis=0, tiled=True, axis_index_groups=groups
    ).reshape(width // 2, hidden_chip)
    def compact(pieces, values):
        count = len(pieces) * far * capacity
        out_width = width + 128 + (classes if values else 0)
        return call(
            functools.partial(compact_kernel, len(pieces), gates, capacity),
            [struct((count, out_width), bf16)] * 2,
            [got[0], *pieces, *values],
            limit=SMALL,
        )

    def scenario_forward(pieces):
        count = len(pieces) * far * capacity
        x_own, x_send = compact(pieces, [])
        out_own, out_send = call(
            functools.partial(scenario_forward_kernel, hidden),
            [struct((count, width), bf16)] * 2,
            [x_own, send(x_send, 1), widen, narrow],
            scratch=[pltpu.VMEM((2 * count, slot_width), bf16)],
            limit=SMALL,
        )
        return out_own, send(out_send, 1)

    mixing_home = scenario_forward(got[:1])
    got[1], mixing_home, w1a = lax.optimization_barrier((got[1], mixing_home, w1a))
    mixing_away = scenario_forward(got[1:])
    out_own, reduce_other = lax.optimization_barrier((mixing_away[0], reduce_other))
    mixing_away = (out_own, mixing_away[1])
    (w2,) = call(
        join_units_kernel,
        [struct((hidden_chip, width), bf16)],
        [reduce, reduce_other],
        limit=SMALL,
    )
    w1b = send(w1a, 1)
    weights = [w1a, w1b, w2]
    weight_scratch = [pltpu.VMEM((width, hidden_chip), bf16)]

    def forward(pieces, mixing, lines):
        count = len(pieces) * far
        return call(
            functools.partial(shared_forward_kernel, len(pieces), lines[0], lanes, gates, depth),
            [struct((len(pieces) * line, rows, width), bf16) for line in lines],
            [got[0], *pieces, *weights, *mixing],
            scratch=[
                pltpu.VMEM((count * rows, width), bf16),
                pltpu.VMEM((count * rows, AUX), bf16),
                *weight_scratch,
                pltpu.VMEM((count * rows, hidden_chip), bf16),
            ],
            limit=BIG,
        )

    split = far // 2
    lines = (split, far - split)
    away = forward(got[1:], mixing_away, lines)
    (home,) = forward(got[:1], mixing_home, (far,))

    def along_near(home, away):
        count = home.shape[0]
        total = home.astype(f32)
        for a in range(1, near):
            total = total + send(away[(a - 1) * count : a * count], 2 * a).astype(f32)
        return total.astype(bf16)

    def along_far(low, high):
        column = [low[b] for b in range(split)] + [high[b] for b in range(far - split)]
        return [column[0]] + [send(column[b], 2 * near * b) for b in range(1, far)]

    high = along_near(home[split:], away[1])
    low = along_near(home[:split], away[0])
    layer_parts = along_far(low, high)
    logit_grad, head_part = call(
        functools.partial(head_kernel, len(layer_parts)),
        [struct((rows, classes), bf16), struct((width, classes), f32)],
        [*layer_parts, head, mentor],
        limit=8,
    )
    logits = gather(logit_grad)
    masks = [2**i for i in range(devices.bit_length() - 2, 0, -1)]
    head_part = total_of(head_part + send(head_part, 1), masks[:1])
    logits[0], head_part = lax.optimization_barrier((logits[0], head_part))

    x_own, x_send = compact(got, logits)
    logits[0], x_send = lax.optimization_barrier((logits[0], x_send))
    x_other = send(x_send, 1)
    dx, mix, dw1_keep, dw1_send, dw2_keep, dw2_send = call(
        functools.partial(shared_backward_kernel, n, lanes, depth),
        [
            struct((all_rows, width), bf16),
            struct((all_rows, AUX), f32),
            struct((width // 2, hidden_chip), bf16),
            struct((width // 2, hidden_chip), bf16),
            struct((shared, lanes // 2, width), bf16),
            struct((shared, lanes // 2, width), bf16),
        ],
        [*got, *logits, head, *weights],
        scratch=[
            pltpu.VMEM((all_rows, width), bf16),
            pltpu.VMEM((width, all_rows), bf16),
            pltpu.VMEM((all_rows, AUX), bf16),
            *weight_scratch,
            pltpu.VMEM((all_rows, width), bf16),
            pltpu.VMEM((all_rows, hidden_chip), bf16),
            pltpu.VMEM((all_rows, min(256, hidden_chip)), bf16),
        ],
        limit=BIG,
    )
    dw1 = (dw1_keep.astype(f32) + send(dw1_send, 1).astype(f32)).astype(bf16)
    dw1, x_own = lax.optimization_barrier((dw1, x_own))
    dw1 = lax.all_to_all(
        dw1.reshape(chips, depth, hidden_chip),
        AXIS, split_axis=0, concat_axis=0, tiled=True, axis_index_groups=groups,
    )
    dx_own, dx_send, widen_grad, narrow_grad = call(
        functools.partial(scenario_backward_kernel, hidden),
        [struct((slots, width + 128), bf16)] * 2
        + [struct((width, slot_width), f32), struct((slot_width, width), f32)],
        [x_own, x_other, head, widen, narrow],
        None,
        [
            pltpu.VMEM((2 * slots, width + 128 + classes), bf16),
            pltpu.VMEM((width, 2 * slots), bf16),
            pltpu.VMEM((2 * slots, width), bf16),
            pltpu.VMEM((2 * slots, slot_width), bf16),
            pltpu.VMEM((2 * slots, min(TILE, slot_width)), bf16),
            pltpu.VMEM((2 * slots, 128), f32),
        ],
        limit=BIG,
    )
    dx_other = send(dx_send, 1)
    dw2_came = send(dw2_send, 1)
    grad_home, low, high, mix = call(
        functools.partial(scatter_kernel, n, split, gates),
        [
            struct((far, pack_rows, width), bf16),
            *[struct(((near - 1) * line, pack_rows, width), bf16) for line in lines],
            struct((chips, AUX, rows), bf16),
        ],
        [*got, dx, mix, dx_own, dx_other],
        limit=SMALL,
    )
    (gate_part,) = call(
        functools.partial(gate_kernel, n, gates),
        [struct((2 * gates * scenarios, width // 2), f32)],
        [*got, mix],
        limit=SMALL,
    )
    gate_part = gate_part + send(gate_part, 1)
    count = gate_part.shape[0]
    joined = classes == width // 2
    low, high, gate_part, dw1 = lax.optimization_barrier((low, high, gate_part, dw1))
    high = along_near(grad_home[split:], high)
    low = along_near(grad_home[:split], low)
    low, dw2_keep = lax.optimization_barrier((low, dw2_keep))
    grad_parts = along_far(low, high)
    reduce_grad = dw2_keep.astype(f32) + dw2_came.astype(f32)
    gate_part = total_of(gate_part, masks[:1])
    if joined:
        value = total_of(jnp.concatenate([gate_part, head_part]), masks[1:-1])
        kept = value.astype(bf16)
        came = send(kept, masks[-1])
        gate_total = kept[:count].astype(f32) + came[:count].astype(f32)
        head_total = kept[count:].astype(f32) + came[count:].astype(f32)
    else:
        gate_total = total_of(gate_part, masks[1:])
        head_total = total_of(head_part, masks[1:])
    halves = [gate_total[: count // 2], gate_total[count // 2 :]]
    gate_total = jnp.concatenate(halves, axis=1).reshape(gates, scenarios, width)
    gate_total = jnp.transpose(gate_total, (1, 2, 0))
    if tiled:
        (expand_grad,) = call(
            expand_grad_kernel, [struct((shared, depth, hidden), f32)], [dw1], limit=8
        )
    else:
        expand_grad = dw1.reshape(chips, depth, shared, lanes).transpose(2, 1, 0, 3)
        expand_grad = expand_grad.reshape(shared, depth, hidden).astype(f32)

    grad_parts, gate_total, head_total = lax.optimization_barrier(
        (grad_parts, gate_total, head_total)
    )
    (feature_grad,) = call(
        functools.partial(final_kernel, len(grad_parts), gates),
        [struct((rows, width), bf16)],
        [*grad_parts, features, sid, probs, gate],
        limit=8,
    )
    return (
        feature_grad,
        expand_grad,
        reduce_grad,
        widen_grad[None],
        narrow_grad[None],
        gate_total,
        head_total,
    )


def solution(mesh):
    placed = (
        P(("groups", "expert"), None),
        P(("groups", "expert")),
        P("groups"),
        P(),
        P(("groups", "expert"), None),
        P(),
        P(None, "expert", None),
        P(None, "expert", None),
        P("expert", None, None),
        P("expert", None, None),
        P(),
    )
    return jax.shard_map(
        body,
        mesh=mesh,
        in_specs=placed,
        out_specs=(
            P(("groups", "expert"), None),
            P("groups", "expert", None),
            P("groups", "expert", None),
            P(("groups", "expert"), None, None),
            P(("groups", "expert"), None, None),
            P("groups", None, None),
            P("groups", None),
        ),
        check_vma=False,
    )
```
